256 devices in a mesh: row: 8 (over x, core), col: 32 (over z, y).
Axes of the slice: x: 4, y: 4, z: 8, core: 2. Of those that a mesh axis runs over, the one named last changes fastest.
Arguments:
- centres: float32 [524288, 64], P(('row', 'col')), may hold values from -6 to 6
- weights: float32 [524288, 64], P(('row', 'col')), may hold values from -0.078125 to 0.078125
- targets: float32 [512, 64], replicated, may hold values from -6 to 6
- batch_index: int32 [512], replicated, may hold values from 0 to 524287
- nystrom_index: int32 [4096], replicated, may hold values from 0 to 524287
- eigvecs: float32 [4096, 1024], P('row', 'col'), may hold values from -0.09375 to 0.09375
- mode_scale: float32 [1024], P('col'), may hold values from 0.02 to 0.2
Outputs:
- residual: float32 [512, 64], replicated
- step: float32 [524288, 64], P(('row', 'col'))
The draws below stay inside these ranges and needn't reach their ends.
All inputs are finite; a program needn't handle non-finite values.
Results may differ from the reference program's by a relative error of at most 0.0001.
Values sent between devices are 32-bit elements; how exact they have to be, the bound alone decides.
No kernel may reach another device: no remote copies, remote signals or barrier semaphores. Data moves between devices by JAX's collectives and lax.ppermute only.
A program may use at most 128 MiB of HBM per device.

```python
import math
import jax
import jax.numpy as jnp
from jax import lax

F = 64
O = 64
M = 4096
Q = 1024
B = 512
P_DEV = 2048
CENTRES = 524288


def set_ends(result, stream_key, least, top_value):
    shape = result.shape
    spot = [jax.random.randint(jax.random.fold_in(stream_key, axis), (), 0, shape[axis]) for axis in range(len(shape))]
    result = result.at[tuple(spot)].set(least)
    longest = shape.index(max(shape))
    spot[longest] = (spot[longest] + 1) % shape[longest]
    return result.at[tuple(spot)].set(top_value)


def level_of(key, dims, cuts, low, top_value):
    def one(axis_at, parts):
        steps = jax.random.uniform(jax.random.fold_in(jax.random.fold_in(key, 6), axis_at), (parts,), jnp.float32, low / len(cuts), top_value / len(cuts))
        return jnp.repeat(jnp.exp(steps), dims[axis_at] // parts).reshape((-1,) + (1,) * (len(dims) - axis_at - 1))

    level = one(*cuts[0])
    for cut in cuts[1:]:
        level = level * one(*cut)
    return level


def gaussian(key, shape, deviation, reach, pieces=(), dtype=jnp.bfloat16):
    result = deviation * jax.random.normal(key, shape, jnp.float32)
    if pieces:
        result = result * level_of(key, shape, pieces, -0.22, 0.18)
    return jnp.clip(result, -reach, reach).astype(dtype)


def setup_inputs(seed: int = 0) -> dict:
    streams_of = jax.random.split(jax.random.key(seed), 8)
    centres = gaussian(streams_of[0], (CENTRES, F), 1.0, 6.0, ((0, 256),), jnp.float32)
    weights = gaussian(streams_of[1], (CENTRES, O), (4.0 / CENTRES ** 0.5), 0.078125, ((0, 256),), jnp.float32)
    targets = gaussian(streams_of[2], (B, O), 1.0, 6.0, (), jnp.float32)
    batch_index = set_ends(jax.random.randint(streams_of[3], (B,), 0, CENTRES), jax.random.fold_in(streams_of[3], 1), 0, CENTRES - 1).astype(jnp.int32)
    nystrom_index = set_ends(jax.random.randint(streams_of[4], (M,), 0, CENTRES), jax.random.fold_in(streams_of[4], 1), 0, CENTRES - 1).astype(jnp.int32)
    eigvecs = gaussian(streams_of[5], (M, Q), M ** -0.5, 0.09375, ((0, 8), (1, 32)), jnp.float32)
    mode_scale = jnp.clip(jnp.exp(math.log(0.2) - 2.3025851 * jax.random.uniform(streams_of[6], (Q,), jnp.float32) ** level_of(streams_of[6], (Q,), ((0, 32),), -0.2, 0.2)), 0.02, 0.2)
    return {"centres": centres, "weights": weights, "targets": targets, "batch_index": batch_index, "nystrom_index": nystrom_index, "eigvecs": eigvecs, "mode_scale": mode_scale}


learning_rate = 0.25


def kernel(left, right):
    left_sq = jnp.sum(left * left, axis=1)
    right_sq = jnp.sum(right * right, axis=1)
    inner_prod = jnp.dot(left, right.T, precision=lax.Precision.HIGHEST, preferred_element_type=jnp.float32)
    return jnp.exp(-(left_sq[:, None] + right_sq[None, :] - 2.0 * inner_prod) / float(F))


def reference(centres, weights, targets, batch_index, nystrom_index, eigvecs, mode_scale):
    batch_feats = centres[batch_index]
    nystrom = centres[nystrom_index]
    blocks = CENTRES // P_DEV
    cent_blocks = centres.reshape(blocks, P_DEV, F)
    wts_blocks = weights.reshape(blocks, P_DEV, O)

    def add_block(running, pair):
        cent_blk, wts_blk = pair
        kern_tile = kernel(cent_blk, batch_feats)
        return running + jnp.dot(kern_tile.T, wts_blk, precision=lax.Precision.HIGHEST, preferred_element_type=jnp.float32), None

    prediction, unused = lax.scan(add_block, jnp.zeros((B, O), jnp.float32), (cent_blocks, wts_blocks))
    residual = prediction - targets
    gradient = jnp.dot(kernel(nystrom, batch_feats), residual, precision=lax.Precision.HIGHEST, preferred_element_type=jnp.float32)
    coeff = mode_scale[:, None] * jnp.dot(eigvecs.T, gradient, precision=lax.Precision.HIGHEST, preferred_element_type=jnp.float32)
    correction = jnp.dot(eigvecs, coeff, precision=lax.Precision.HIGHEST, preferred_element_type=jnp.float32)

    def step_block(cent_blk):
        direct = jnp.dot(kernel(cent_blk, batch_feats), residual, precision=lax.Precision.HIGHEST, preferred_element_type=jnp.float32)
        back = jnp.dot(kernel(cent_blk, nystrom), correction, precision=lax.Precision.HIGHEST, preferred_element_type=jnp.float32)
        return learning_rate * (direct - back)

    step = lax.map(step_block, cent_blocks).reshape(CENTRES, O)
    return residual, step
```

```python
import functools

import jax
import jax.numpy as jnp
from jax import lax
from jax.experimental import pallas as pl
from jax.experimental.pallas import tpu as pltpu
from jax.sharding import Mesh
from jax.sharding import PartitionSpec as P

F32 = jnp.float32
BF16 = jnp.bfloat16
ROW = ("x", "core")
COL = ("z", "y")
CHIPS = ("x", "z", "y")
ALL = ("x", "core", "z", "y")
NX, NCORE, NROW, NCOL, NCHIPS = 4, 2, 8, 32, 128
FEATS, OUTS, BATCH, NYS, MODES = 64, 64, 512, 4096, 32
PDEV = 2048
RATE = 0.25
MIB = 1024 * 1024


def params(mib=48, grid=1):
    return pltpu.CompilerParams(
        vmem_limit_bytes=mib * MIB, dimension_semantics=("arbitrary",) * grid
    )


def cost(flops, nbytes, trans=0):
    return pl.CostEstimate(flops=int(flops), bytes_accessed=int(nbytes), transcendentals=int(trans))


def dot(a, b):
    return lax.dot_general(a, b, (((1,), (0,)), ((), ())), preferred_element_type=F32)


def dot_nt(a, b):
    return lax.dot_general(a, b, (((1,), (1,)), ((), ())), preferred_element_type=F32)


def split2(v):
    hi = v.astype(BF16)
    lo = (v - hi.astype(F32)).astype(BF16)
    return hi, lo


def split3(v):
    hi = v.astype(BF16).astype(F32)
    rest = v - hi
    mid = rest.astype(BF16).astype(F32)
    low = (rest - mid).astype(BF16).astype(F32)
    return hi, mid, low


def kern(a, bt):
    ah, am, al = split3(a)
    bh, bm, bl = split3(bt)
    a1 = jnp.concatenate([ah, ah, am], axis=1).astype(BF16)
    a2 = jnp.concatenate([am, ah, al], axis=1).astype(BF16)
    b1 = jnp.concatenate([bh, bm, bh], axis=0).astype(BF16)
    b2 = jnp.concatenate([bm, bl, bh], axis=0).astype(BF16)
    inner = dot(a1, b1) + dot(a2, b2)
    asq = jnp.sum(a * a, axis=1, keepdims=True)
    bsq = jnp.sum(bt * bt, axis=0, keepdims=True)
    return jnp.exp((asq + bsq - 2.0 * inner) * (-1.0 / FEATS))


def select_kernel(index_ref, cent_ref, out_ref, parts):
    @pl.when(pl.program_id(0) == 0)
    def _():
        hi, mid, low = split3(cent_ref[...].T)
        parts[...] = jnp.concatenate([hi, mid, low], axis=0).astype(BF16)

    width = out_ref.shape[1]
    place = lax.broadcasted_iota(jnp.int32, (PDEV, width), 0)
    chosen = jnp.where(place == index_ref[...], 1.0, 0.0).astype(BF16)
    found = dot(parts[...], chosen)
    out_ref[...] = found[:FEATS] + found[FEATS : 2 * FEATS] + found[2 * FEATS :]


def select(index, centres):
    n = index.shape[1]
    block = 512
    return pl.pallas_call(
        select_kernel,
        grid=(n // block,),
        in_specs=[
            pl.BlockSpec((1, block), lambda i: (0, i)),
            pl.BlockSpec((PDEV, FEATS), lambda i: (0, 0)),
        ],
        out_specs=pl.BlockSpec((FEATS, block), lambda i: (0, i)),
        out_shape=jax.ShapeDtypeStruct((FEATS, n), F32),
        scratch_shapes=[pltpu.VMEM((3 * FEATS, PDEV), BF16)],
        compiler_params=params(),
        cost_estimate=cost(2 * 192 * PDEV * n, PDEV * 256 + n * 256),
        name="select",
    )(index, centres)


def add_spread_kernel(in_ref, out_ref):
    total = in_ref[0]
    for i in range(1, in_ref.shape[0]):
        total = total + in_ref[i]
    for i in range(out_ref.shape[0]):
        out_ref[i] = total


def add_spread(parts, copies):
    return pl.pallas_call(
        add_spread_kernel,
        out_shape=jax.ShapeDtypeStruct((copies,) + parts.shape[1:], F32),
        compiler_params=params(grid=0),
        cost_estimate=cost(parts.size, parts.size * 4 + parts.size // parts.shape[0] * copies * 4),
        name="add_spread",
    )(parts)


def add_tiles_kernel(in_ref, out_ref):
    total = in_ref[0]
    for i in range(1, in_ref.shape[0]):
        total = total + in_ref[i]
    for c in range(NCOL):
        out_ref[c] = total[:, c * 128 : (c + 1) * 128]


def add_tiles(parts):
    return pl.pallas_call(
        add_tiles_kernel,
        out_shape=jax.ShapeDtypeStruct((NCOL, 8, 128), F32),
        compiler_params=params(grid=0),
        cost_estimate=cost(parts.size, parts.size * 5),
        name="add_tiles",
    )(parts)


def place_tiles(core_ref, own_ref, other_ref, out_ref):
    mine = core_ref[0]
    for x in range(NX):
        for part, core in ((own_ref, mine), (other_ref, 1 - mine)):
            at = pl.multiple_of((2 * x + core) * 8, 8)
            for c in range(NCOL):
                out_ref[pl.ds(at, 8), c * 128 : (c + 1) * 128] = part[x * NCOL + c]


def assemble(core, own, other):
    return pl.pallas_call(
        place_tiles,
        in_specs=[
            pl.BlockSpec(memory_space=pltpu.SMEM),
            pl.BlockSpec(memory_space=pltpu.VMEM),
            pl.BlockSpec(memory_space=pltpu.VMEM),
        ],
        out_shape=jax.ShapeDtypeStruct((FEATS, NYS), F32),
        compiler_params=params(grid=0),
        cost_estimate=cost(0, 2 * MIB),
        name="assemble",
    )(core, own, other)


def batch_kernel(cent_ref, batch_ref, wts_ref, pred_ref, hi_ref, lo_ref):
    k = kern(cent_ref[...], batch_ref[...])
    khi, klo = split2(k)
    hi_ref[...] = khi
    lo_ref[...] = klo
    whi, wlo = split2(wts_ref[...].T)
    both = dot(jnp.concatenate([whi, wlo], axis=0), khi)
    part = both[:OUTS] + both[OUTS:] + dot(whi, klo)

    @pl.when(pl.program_id(0) == 0)
    def _():
        pred_ref[...] = part

    @pl.when(pl.program_id(0) > 0)
    def _():
        pred_ref[...] += part


def batch_products(centres, batch_t, weights):
    rows = 512
    return pl.pallas_call(
        batch_kernel,
        grid=(PDEV // rows,),
        in_specs=[
            pl.BlockSpec((rows, FEATS), lambda i: (i, 0)),
            pl.BlockSpec((FEATS, BATCH), lambda i: (0, 0)),
            pl.BlockSpec((rows, OUTS), lambda i: (i, 0)),
        ],
        out_specs=[
            pl.BlockSpec((OUTS, BATCH), lambda i: (0, 0)),
            pl.BlockSpec((rows, BATCH), lambda i: (i, 0)),
            pl.BlockSpec((rows, BATCH), lambda i: (i, 0)),
        ],
        out_shape=[
            jax.ShapeDtypeStruct((OUTS, BATCH), F32),
            jax.ShapeDtypeStruct((PDEV, BATCH), BF16),
            jax.ShapeDtypeStruct((PDEV, BATCH), BF16),
        ],
        compiler_params=params(),
        cost_estimate=cost(6e9, 6 * MIB, PDEV * BATCH),
        name="batch_products",
    )(centres, batch_t, weights)


def modes_kernel(batch_ref, nys_ref, eig_ref, scale_ref, out_ref):
    k = kern(batch_ref[...].T, nys_ref[...])
    khi, klo = split2(k)
    ehi, elo = split2(eig_ref[0])
    part = dot_nt(khi, ehi) + dot_nt(khi, elo) + dot_nt(klo, ehi)
    step = pl.program_id(0)

    @pl.when(step == 0)
    def _():
        out_ref[...] = part

    @pl.when(step > 0)
    def _():
        out_ref[...] += part

    @pl.when(step == NROW - 1)
    def _():
        out_ref[...] = out_ref[...] * scale_ref[...]


def mode_products(batch_t, nys_t, eig, scale):
    block = NYS // NROW
    return pl.pallas_call(
        modes_kernel,
        grid=(NROW,),
        in_specs=[
            pl.BlockSpec((FEATS, BATCH), lambda i: (0, 0)),
            pl.BlockSpec((FEATS, block), lambda i: (0, i)),
            pl.BlockSpec((1, MODES, block), lambda i: (i, 0, 0)),
            pl.BlockSpec((1, MODES), lambda i: (0, 0)),
        ],
        out_specs=pl.BlockSpec((BATCH, MODES), lambda i: (0, 0)),
        out_shape=jax.ShapeDtypeStruct((BATCH, MODES), F32),
        compiler_params=params(),
        cost_estimate=cost(1e10, 3 * MIB, NYS * BATCH),
        name="mode_products",
    )(batch_t, nys_t, eig, scale)


def nys_kernel(cent_ref, nys_ref, hi_ref, lo_ref):
    khi, klo = split2(kern(cent_ref[...], nys_ref[...]))
    hi_ref[...] = khi
    lo_ref[...] = klo


def nys_parts(centres, nys_t):
    rows, block = 512, 1024
    shape = jax.ShapeDtypeStruct((PDEV, NYS), BF16)
    return pl.pallas_call(
        nys_kernel,
        grid=(PDEV // rows, NYS // block),
        in_specs=[
            pl.BlockSpec((rows, FEATS), lambda i, j: (i, 0)),
            pl.BlockSpec((FEATS, block), lambda i, j: (0, j)),
        ],
        out_specs=[pl.BlockSpec((rows, block), lambda i, j: (i, j))] * 2,
        out_shape=[shape, shape],
        compiler_params=params(grid=2),
        cost_estimate=cost(1.8e10, 34 * MIB, PDEV * NYS),
        name="nys_parts",
    )(centres, nys_t)


def correct_kernel(pred_ref, targ_ref, modes_ref, eig_ref, resid_ref, tiles_ref):
    total = pred_ref[0]
    for i in range(1, NCOL):
        total = total + pred_ref[i]
    resid = total - targ_ref[...]
    for i in range(NROW):
        resid_ref[i] = resid
    coeff = jnp.dot(
        resid, modes_ref[...], precision=lax.Precision.HIGHEST, preferred_element_type=F32
    )
    per = NCOL // NROW
    for r in range(NROW):
        share = jnp.dot(
            coeff, eig_ref[r], precision=lax.Precision.HIGHEST, preferred_element_type=F32
        )
        for k in range(per):
            tiles_ref[r * per + k] = share[:, k * 128 : (k + 1) * 128]


def correct(pred, targ, modes, eig):
    return pl.pallas_call(
        correct_kernel,
        out_shape=[
            jax.ShapeDtypeStruct((NROW, 8, BATCH), F32),
            jax.ShapeDtypeStruct((NCOL, 8, 128), F32),
        ],
        compiler_params=params(grid=0),
        cost_estimate=cost(1e8, 2 * MIB),
        name="correct",
    )(pred, targ, modes, eig)


def direct_kernel(hi_ref, lo_ref, resid_ref, out_ref, outr_ref):
    rhi, rlo = split2(resid_ref[...])
    out_ref[...] = dot_nt(hi_ref[...], rhi) + dot_nt(hi_ref[...], rlo) + dot_nt(lo_ref[...], rhi)
    outr_ref[...] = resid_ref[...].T


def direct_part(hi, lo, resid_t):
    return pl.pallas_call(
        direct_kernel,
        out_shape=[
            jax.ShapeDtypeStruct((PDEV, OUTS), F32),
            jax.ShapeDtypeStruct((BATCH, OUTS), F32),
        ],
        compiler_params=params(grid=0),
        cost_estimate=cost(1e9, 5 * MIB),
        name="direct_part",
    )(hi, lo, resid_t)


def step_kernel(core_ref, own_ref, other_ref, hi_ref, lo_ref, direct_ref, out_ref, corr, parts):
    @pl.when(pl.program_id(0) == 0)
    def _():
        place_tiles(core_ref, own_ref, other_ref, corr)
        hi, lo = split2(corr[...])
        parts[:OUTS] = hi
        parts[OUTS:] = lo

    both = dot_nt(hi_ref[...], parts[...])
    back = both[:, :OUTS] + both[:, OUTS:] + dot_nt(lo_ref[...], parts[:OUTS])
    out_ref[...] = RATE * (direct_ref[...] - back)


def step_of(core, own, other, hi, lo, direct):
    rows = 256
    whole = pl.BlockSpec((NCHIPS, 8, 128), lambda i: (0, 0, 0))
    return pl.pallas_call(
        step_kernel,
        grid=(PDEV // rows,),
        in_specs=[
            pl.BlockSpec(memory_space=pltpu.SMEM),
            whole,
            whole,
            pl.BlockSpec((rows, NYS), lambda i: (i, 0)),
            pl.BlockSpec((rows, NYS), lambda i: (i, 0)),
            pl.BlockSpec((rows, OUTS), lambda i: (i, 0)),
        ],
        out_specs=pl.BlockSpec((rows, OUTS), lambda i: (i, 0)),
        out_shape=jax.ShapeDtypeStruct((PDEV, OUTS), F32),
        scratch_shapes=[pltpu.VMEM((OUTS, NYS), F32), pltpu.VMEM((2 * OUTS, NYS), BF16)],
        compiler_params=params(),
        cost_estimate=cost(1.2e10, 36 * MIB),
        name="step_of",
    )(core, own, other, hi, lo, direct)


def swap(parts, axes):
    return lax.all_to_all(parts, axes, 0, 0, tiled=True)


def to_all(tiles):
    own = swap(tiles, CHIPS)
    other = lax.ppermute(own, "core", [(0, 1), (1, 0)])
    return own, other


def local(centres, weights, targets, batch_index, nystrom_index, eigvecs, mode_scale):
    offset = lax.axis_index(ALL) * PDEV
    core = jnp.full((1,), lax.axis_index("core"), jnp.int32)
    row = lax.axis_index(ROW)

    feats = select((batch_index - offset)[None, :], centres)
    feats = swap(feats.reshape(NROW, 8, BATCH), ROW)
    feats = swap(add_spread(feats, NCOL), COL)
    feats = swap(add_spread(feats, NROW), ROW)
    batch_t = feats.reshape(FEATS, BATCH)

    eig = swap(jnp.broadcast_to(eigvecs.T[None], (NROW, MODES, NYS // NROW)), ROW)

    nys = select((nystrom_index - offset)[None, :], centres)
    nys = swap(nys.reshape(NROW, 8, NYS), ROW)
    nys = swap(add_tiles(nys), COL)
    nys_t = assemble(core, *to_all(add_spread(nys, NCHIPS)))

    pred, khi, klo = batch_products(centres, batch_t, weights)
    pred = swap(pred.reshape(NROW, 8, BATCH), ROW)
    pred = swap(add_spread(pred, NCOL), COL)

    modes = mode_products(batch_t, nys_t, eig, mode_scale[None, :])
    targ = lax.dynamic_slice_in_dim(targets, row * 8, 8, 1).T
    resid, tiles = correct(pred, targ, modes, eig)
    tiles = swap(tiles, COL)
    own, other = to_all(add_spread(tiles, NCHIPS))

    nhi, nlo = nys_parts(centres, nys_t)
    resid_t = swap(resid, ROW).reshape(OUTS, BATCH)
    direct, residual = direct_part(khi, klo, resid_t)
    step = step_of(core, own, other, nhi, nlo, direct)
    return residual, step


def solution(mesh):
    fine = Mesh(mesh.devices.reshape(NX, NCORE, 8, 4), ALL)
    in_specs = (
        P(ALL, None),
        P(ALL, None),
        P(),
        P(),
        P(),
        P(ROW, COL),
        P(COL),
    )
    out_specs = (P(), P(ALL, None))
    return jax.shard_map(local, mesh=fine, in_specs=in_specs, out_specs=out_specs, check_vma=False)
```

```python
import functools

import jax
import jax.numpy as jnp
from jax import lax
from jax.experimental import pallas as pl
from jax.experimental.pallas import tpu as pltpu
from jax.sharding import Mesh
from jax.sharding import PartitionSpec as P

F32 = jnp.float32
BF16 = jnp.bfloat16
ROW = ("x", "core")
COL = ("z", "y")
CHIPS = ("x", "z", "y")
ALL = ("x", "core", "z", "y")
NX, NCORE, NROW, NCOL, NCHIPS = 4, 2, 8, 32, 128
FEATS, OUTS, BATCH, NYS, MODES = 64, 64, 512, 4096, 32
PDEV = 2048
SHIFT = 11
SLOTS, SLOTROWS = 64, 16
PARTS = 2
RATE = 0.25
MIB = 1024 * 1024


def params(mib=24, grid=1):
    return pltpu.CompilerParams(
        vmem_limit_bytes=mib * MIB, dimension_semantics=("arbitrary",) * grid
    )


def cost(flops, nbytes, trans=0):
    return pl.CostEstimate(flops=int(flops), bytes_accessed=int(nbytes), transcendentals=int(trans))


def dot(a, b):
    return lax.dot_general(a, b, (((1,), (0,)), ((), ())), preferred_element_type=F32)


def dot_nt(a, b):
    return lax.dot_general(a, b, (((1,), (1,)), ((), ())), preferred_element_type=F32)


def split2(v):
    hi = v.astype(BF16)
    lo = (v - hi.astype(F32)).astype(BF16)
    return hi, lo


def split3(v):
    hi = v.astype(BF16).astype(F32)
    rest = v - hi
    mid = rest.astype(BF16).astype(F32)
    low = (rest - mid).astype(BF16).astype(F32)
    return hi, mid, low


def kern(a, bt):
    ah, am, al = split3(a)
    bh, bm, bl = split3(bt)
    a1 = jnp.concatenate([ah, ah, am], axis=1).astype(BF16)
    a2 = jnp.concatenate([am, ah, al], axis=1).astype(BF16)
    b1 = jnp.concatenate([bh, bm, bh], axis=0).astype(BF16)
    b2 = jnp.concatenate([bm, bl, bh], axis=0).astype(BF16)
    inner = dot(a1, b1) + dot(a2, b2)
    asq = jnp.sum(a * a, axis=1, keepdims=True)
    bsq = jnp.sum(bt * bt, axis=0, keepdims=True)
    return jnp.exp((asq + bsq - 2.0 * inner) * (-1.0 / FEATS))


def chip_of(index):
    owner = lax.shift_right_logical(index, SHIFT)
    return lax.shift_right_logical(owner, 6) * NCOL + (owner & (NCOL - 1))


def core_of(index):
    return lax.shift_right_logical(index, SHIFT + 5) & 1


def pack_kernel(core_ref, chip_ref, index_ref, cent_ref, keep_ref, send_ref):
    rows = index_ref.shape[0]
    index = index_ref[...]
    ours = chip_of(index) == chip_ref[0]
    ones = jnp.where(ours, 1.0, 0.0).astype(BF16)
    lane_from = lax.broadcasted_iota(jnp.int32, (128, 128), 0)
    lane_to = lax.broadcasted_iota(jnp.int32, (128, 128), 1)
    in_row = dot(ones, jnp.where(lane_from < lane_to, 1.0, 0.0).astype(BF16))
    row_to = lax.broadcasted_iota(jnp.int32, (rows, rows), 0)
    row_from = lax.broadcasted_iota(jnp.int32, (rows, rows), 1)
    before = dot(jnp.where(row_from < row_to, 1.0, 0.0).astype(BF16), ones)
    rank = in_row + jnp.sum(before, axis=1, keepdims=True)
    rank = jnp.where(ours & (core_of(index) == core_ref[0]), rank, -1.0)
    local_row = (index & (PDEV - 1)).astype(F32) + 1.0

    slot = lax.broadcasted_iota(jnp.int32, (SLOTS, 128), 0).astype(F32)
    found = jnp.zeros((SLOTS, 128), F32)
    for i in range(rows):
        found += jnp.where(rank[i : i + 1] == slot, local_row[i : i + 1], 0.0)
    source = jnp.sum(found, axis=1, keepdims=True).astype(jnp.int32) - 1
    place = lax.broadcasted_iota(jnp.int32, (SLOTS, PDEV), 1)
    chosen = jnp.where(place == source, 1.0, 0.0).astype(BF16)
    hi, mid, low = split3(cent_ref[...])
    parts = jnp.concatenate([hi, mid, low], axis=0).astype(BF16)
    got = dot_nt(chosen, parts)
    got = got[:, :FEATS] + got[:, FEATS : 2 * FEATS] + got[:, 2 * FEATS :]
    n = SLOTROWS
    zero = jnp.concatenate([got[:n], got[n : 2 * n]], axis=1)
    one = jnp.concatenate([got[2 * n : 3 * n], got[3 * n :]], axis=1)
    at_zero = core_ref[0] == 0
    keep_ref[...] = jnp.where(at_zero, zero, one)
    send_ref[...] = jnp.where(at_zero, one, zero)


def pack(core, chip, index, cent_t):
    smem = pl.BlockSpec(memory_space=pltpu.SMEM)
    vmem = pl.BlockSpec(memory_space=pltpu.VMEM)
    shape = jax.ShapeDtypeStruct((SLOTROWS, 128), F32)
    return pl.pallas_call(
        pack_kernel,
        in_specs=[smem, smem, vmem, vmem],
        out_shape=[shape, shape],
        compiler_params=params(grid=0),
        cost_estimate=cost(1e9, 2 * MIB),
        name="pack",
    )(core, chip, index, cent_t)


def join_spread_kernel(keep_ref, came_ref, out_ref):
    message = keep_ref[...] + came_ref[...]
    for i in range(out_ref.shape[0]):
        out_ref[i] = message


def join_spread(keep, came):
    return pl.pallas_call(
        join_spread_kernel,
        out_shape=jax.ShapeDtypeStruct((NCHIPS,) + keep.shape, F32),
        compiler_params=params(grid=0),
        cost_estimate=cost(0, MIB),
        name="join_spread",
    )(keep, came)


def across_rows(row):
    return jnp.broadcast_to(row.astype(F32), (128, row.shape[1])).T


def batch_slots_kernel(core_ref, batch_ref, nys_ref, out_ref):
    index = batch_ref[...]
    chip = chip_of(index)
    source = lax.broadcasted_iota(jnp.int32, (BATCH, 128), 0)
    lane = lax.broadcasted_iota(jnp.int32, (BATCH, 128), 1)
    from_batch = across_rows(chip)
    from_nys = across_rows(chip_of(nys_ref[...]))
    for k in range(BATCH // 128):
        here = chip[:, k * 128 : (k + 1) * 128]
        target = here.astype(F32)
        ahead = (from_batch == target) & (source < lane + k * 128)
        rank = jnp.sum(jnp.where(ahead, 1.0, 0.0), axis=0, keepdims=True)
        rank += jnp.sum(jnp.where(from_nys == target, 1.0, 0.0), axis=0, keepdims=True)
        rank = rank.astype(jnp.int32)
        place = here * SLOTROWS + (rank & (SLOTROWS - 1))
        piece = lax.shift_right_logical(rank, 4)
        for which in range(2):
            core = core_ref[0] if which == 0 else 1 - core_ref[0]
            for half in range(2):
                at = 2 * which + half
                value = jnp.where(piece == 2 * core + half, place, -1)
                out_ref[at : at + 1, k * 128 : (k + 1) * 128] = value


def batch_slots(core, batch_index, nys_index):
    vmem = pl.BlockSpec(memory_space=pltpu.VMEM)
    return pl.pallas_call(
        batch_slots_kernel,
        in_specs=[pl.BlockSpec(memory_space=pltpu.SMEM), vmem, vmem],
        out_shape=jax.ShapeDtypeStruct((4, BATCH), jnp.int32),
        compiler_params=params(grid=0),
        cost_estimate=cost(1e6, MIB),
        name="batch_slots",
    )(core, batch_index, nys_index)


def unpack_batch_kernel(slot_ref, own_ref, other_ref, out_ref, outr_ref):
    chips = 64
    rows = chips * SLOTROWS
    total = jnp.zeros((3 * FEATS, BATCH), F32)
    for which, ref in ((0, own_ref), (1, other_ref)):
        for part in range(NCHIPS // chips):
            block = ref[part * chips : (part + 1) * chips].reshape(rows, 128).T
            hi, mid, low = split3(block)
            place = lax.broadcasted_iota(jnp.int32, (rows, BATCH), 0) + part * rows
            for half in range(2):
                at = slice(half * FEATS, (half + 1) * FEATS)
                parts = jnp.concatenate([hi[at], mid[at], low[at]], axis=0).astype(BF16)
                slot = slot_ref[2 * which + half : 2 * which + half + 1]
                total += dot(parts, jnp.where(place == slot, 1.0, 0.0).astype(BF16))
    feats = total[:FEATS] + total[FEATS : 2 * FEATS] + total[2 * FEATS :]
    out_ref[...] = feats
    outr_ref[...] = feats.T


def unpack_batch(slots, own, other):
    return pl.pallas_call(
        unpack_batch_kernel,
        out_shape=[
            jax.ShapeDtypeStruct((FEATS, BATCH), F32),
            jax.ShapeDtypeStruct((BATCH, FEATS), F32),
        ],
        compiler_params=params(grid=0),
        cost_estimate=cost(1e9, 4 * MIB),
        name="unpack_batch",
    )(slots, own, other)


def unpack_nys_kernel(core_ref, start_ref, own_ref, other_ref, out_ref):
    n = SLOTROWS

    def run(zero_ref, one_ref):
        def body(i, _):
            at = start_ref[i]
            zero, one = zero_ref[i], one_ref[i]
            out_ref[pl.ds(at, n), :] = zero[:, :FEATS]
            out_ref[pl.ds(at + n, n), :] = zero[:, FEATS:]
            out_ref[pl.ds(at + 2 * n, n), :] = one[:, :FEATS]
            out_ref[pl.ds(at + 3 * n, n), :] = one[:, FEATS:]
            return 0

        lax.fori_loop(0, NCHIPS, body, 0, unroll=8)

    @pl.when(core_ref[0] == 0)
    def _():
        run(own_ref, other_ref)

    @pl.when(core_ref[0] == 1)
    def _():
        run(other_ref, own_ref)


def unpack_nys(core, starts, own, other):
    smem = pl.BlockSpec(memory_space=pltpu.SMEM)
    vmem = pl.BlockSpec(memory_space=pltpu.VMEM)
    return pl.pallas_call(
        unpack_nys_kernel,
        in_specs=[smem, smem, vmem, vmem],
        out_shape=jax.ShapeDtypeStruct((NYS + SLOTS, FEATS), F32),
        compiler_params=params(grid=0),
        cost_estimate=cost(0, 8 * MIB),
        name="unpack_nys",
    )(core, starts, own, other)


def order_kernel(index_ref, out_ref, across):
    width = out_ref.shape[1]
    step = pl.program_id(0)
    number = lax.broadcasted_iota(jnp.int32, (1, NYS), 1)
    key = (chip_of(index_ref[...]) * NYS + number).astype(F32)

    @pl.when(step == 0)
    def _():
        across[...] = across_rows(key)

    for i in range(NYS // width):

        @pl.when(step == i)
        def _():
            for k in range(width // 128):
                at = i * width + k * 128
                lower = jnp.where(across[...] < key[:, at : at + 128], 1.0, 0.0)
                count = jnp.sum(lower, axis=0, keepdims=True)
                out_ref[:, k * 128 : (k + 1) * 128] = count.astype(jnp.int32)


def order(index):
    block = 512
    return pl.pallas_call(
        order_kernel,
        grid=(NYS // block,),
        in_specs=[pl.BlockSpec((1, NYS), lambda i: (0, 0))],
        out_specs=pl.BlockSpec((1, block), lambda i: (0, i)),
        out_shape=jax.ShapeDtypeStruct((1, NYS), jnp.int32),
        scratch_shapes=[pltpu.VMEM((NYS, 128), F32)],
        compiler_params=params(),
        cost_estimate=cost(3e9, MIB),
        name="order",
    )(index)


def reorder_kernel(row_ref, order_ref, eig_ref, out_ref, parts):
    width = out_ref.shape[1]
    step = pl.program_id(0)
    block = NYS // NROW

    @pl.when(step == 0)
    def _():
        for i in range(NROW):
            at = pl.multiple_of((row_ref[0] ^ i) * block, block)
            hi, mid, low = split3(eig_ref[i])
            parts[:, pl.ds(at, block)] = jnp.concatenate([hi, mid, low], axis=0).astype(BF16)

    place = lax.broadcasted_iota(jnp.int32, (width, NYS), 0) + step * width
    chosen = jnp.where(place == order_ref[...], 1.0, 0.0).astype(BF16)
    got = dot_nt(parts[...], chosen)
    out_ref[...] = got[:MODES] + got[MODES : 2 * MODES] + got[2 * MODES :]


def reorder(row, orders, eig):
    block = 512
    return pl.pallas_call(
        reorder_kernel,
        grid=(NYS // block,),
        in_specs=[
            pl.BlockSpec(memory_space=pltpu.SMEM),
            pl.BlockSpec((1, NYS), lambda i: (0, 0)),
            pl.BlockSpec((NROW, MODES, NYS // NROW), lambda i: (0, 0, 0)),
        ],
        out_specs=pl.BlockSpec((MODES, block), lambda i: (0, i)),
        out_shape=jax.ShapeDtypeStruct((MODES, NYS), F32),
        scratch_shapes=[pltpu.VMEM((3 * MODES, NYS), BF16)],
        compiler_params=params(),
        cost_estimate=cost(1e10, 2 * MIB),
        name="reorder",
    )(row, orders, eig)


def add_spread_kernel(in_ref, out_ref):
    total = in_ref[0]
    for i in range(1, in_ref.shape[0]):
        total = total + in_ref[i]
    for i in range(out_ref.shape[0]):
        out_ref[i] = total


def add_spread(parts, copies):
    return pl.pallas_call(
        add_spread_kernel,
        out_shape=jax.ShapeDtypeStruct((copies,) + parts.shape[1:], F32),
        compiler_params=params(grid=0),
        cost_estimate=cost(parts.size, parts.size * 4 + parts.size // parts.shape[0] * copies * 4),
        name="add_spread",
    )(parts)


def place_tiles(core_ref, own_ref, other_ref, out_ref):
    mine = core_ref[0]
    for x in range(NX):
        for part, core in ((own_ref, mine), (other_ref, 1 - mine)):
            at = pl.multiple_of((2 * x + core) * 8, 8)
            for c in range(NCOL):
                out_ref[pl.ds(at, 8), c * 128 : (c + 1) * 128] = part[x * NCOL + c]


def batch_kernel(cent_ref, batch_ref, wts_ref, pred_ref):
    khi, klo = split2(kern(batch_ref[...], cent_ref[...]))
    whi, wlo = split2(wts_ref[...])
    both = dot_nt(jnp.concatenate([whi, wlo], axis=0), khi)
    part = both[:OUTS] + both[OUTS:] + dot_nt(whi, klo)

    @pl.when(pl.program_id(0) == 0)
    def _():
        pred_ref[...] = part

    @pl.when(pl.program_id(0) > 0)
    def _():
        pred_ref[...] += part


def batch_products(cent_t, batch_rows, wts_t):
    cols = 512
    return pl.pallas_call(
        batch_kernel,
        grid=(PDEV // cols,),
        in_specs=[
            pl.BlockSpec((FEATS, cols), lambda i: (0, i)),
            pl.BlockSpec((BATCH, FEATS), lambda i: (0, 0)),
            pl.BlockSpec((OUTS, cols), lambda i: (0, i)),
        ],
        out_specs=pl.BlockSpec((OUTS, BATCH), lambda i: (0, 0)),
        out_shape=jax.ShapeDtypeStruct((OUTS, BATCH), F32),
        compiler_params=params(),
        cost_estimate=cost(6e9, 2 * MIB, PDEV * BATCH),
        name="batch_products",
    )(cent_t, batch_rows, wts_t)


def modes_kernel(batch_ref, nys_ref, eig_ref, scale_ref, out_ref):
    khi, klo = split2(kern(nys_ref[...], batch_ref[...]))
    ehi, elo = split2(eig_ref[...])
    both = dot(jnp.concatenate([ehi, elo], axis=0), khi)
    part = both[:MODES] + both[MODES:] + dot(ehi, klo)
    step = pl.program_id(0)

    @pl.when(step == 0)
    def _():
        out_ref[...] = part

    @pl.when(step > 0)
    def _():
        out_ref[...] += part

    @pl.when(step == pl.num_programs(0) - 1)
    def _():
        out_ref[...] = out_ref[...] * scale_ref[...]


def mode_products(batch_t, nys, eig, scale):
    block = 512
    return pl.pallas_call(
        modes_kernel,
        grid=(NYS // block,),
        in_specs=[
            pl.BlockSpec((FEATS, BATCH), lambda i: (0, 0)),
            pl.BlockSpec((block, FEATS), lambda i: (i, 0)),
            pl.BlockSpec((MODES, block), lambda i: (0, i)),
            pl.BlockSpec((MODES, 1), lambda i: (0, 0)),
        ],
        out_specs=pl.BlockSpec((MODES, BATCH), lambda i: (0, 0)),
        out_shape=jax.ShapeDtypeStruct((MODES, BATCH), F32),
        compiler_params=params(),
        cost_estimate=cost(1e10, 3 * MIB, NYS * BATCH),
        name="mode_products",
    )(batch_t, nys, eig, scale)


def nys_kernel(cent_ref, nys_ref, hi_ref, lo_ref):
    khi, klo = split2(kern(nys_ref[...], cent_ref[...]))
    hi_ref[...] = khi
    lo_ref[...] = klo


def nys_parts(cent_t, nys, part):
    rows, block = 1024, 512
    count = NYS // PARTS
    shape = jax.ShapeDtypeStruct((count, PDEV), BF16)
    return pl.pallas_call(
        nys_kernel,
        grid=(count // rows, PDEV // block),
        in_specs=[
            pl.BlockSpec((FEATS, block), lambda i, j: (0, j)),
            pl.BlockSpec((rows, FEATS), lambda i, j: (i + part * (count // rows), 0)),
        ],
        out_specs=[pl.BlockSpec((rows, block), lambda i, j: (i, j))] * 2,
        out_shape=[shape, shape],
        compiler_params=params(56, grid=2),
        cost_estimate=cost(1.8e10 / PARTS, 34 * MIB / PARTS, PDEV * NYS / PARTS),
        name="nys_parts",
    )(cent_t, nys)


def correct_kernel(pred_ref, targ_ref, modes_ref, eig_ref, resid_ref, tiles_ref):
    total = pred_ref[0]
    for i in range(1, NCOL):
        total = total + pred_ref[i]
    resid = total - targ_ref[...]
    resid_ref[...] = resid
    coeff = lax.dot_general(
        resid,
        modes_ref[...],
        (((1,), (1,)), ((), ())),
        precision=lax.Precision.HIGHEST,
        preferred_element_type=F32,
    )
    share = jnp.dot(
        coeff, eig_ref[...], precision=lax.Precision.HIGHEST, preferred_element_type=F32
    )
    for k in range(NCOL):
        tiles_ref[k] = share[:, k * 128 : (k + 1) * 128]


def correct(pred, targ, modes, eig):
    return pl.pallas_call(
        correct_kernel,
        out_shape=[
            jax.ShapeDtypeStruct((8, BATCH), F32),
            jax.ShapeDtypeStruct((NCOL, 8, 128), F32),
        ],
        compiler_params=params(grid=0),
        cost_estimate=cost(1e8, 2 * MIB),
        name="correct",
    )(pred, targ, modes, eig)


def direct_kernel(row_ref, cent_ref, batch_ref, resid_ref, out_ref, outr_ref):
    for i in range(NROW):
        at = pl.multiple_of((row_ref[0] ^ i) * 8, 8)
        outr_ref[pl.ds(at, 8), :] = resid_ref[i]
    khi, klo = split2(kern(batch_ref[...], cent_ref[...]))
    rhi, rlo = split2(outr_ref[...])
    both = dot(jnp.concatenate([rhi, rlo], axis=0), khi)
    out_ref[...] = both[:OUTS] + both[OUTS:] + dot(rhi, klo)


def direct_part(row, cent_t, batch_rows, resid):
    cols = 512
    return pl.pallas_call(
        direct_kernel,
        grid=(PDEV // cols,),
        in_specs=[
            pl.BlockSpec(memory_space=pltpu.SMEM),
            pl.BlockSpec((FEATS, cols), lambda i: (0, i)),
            pl.BlockSpec((BATCH, FEATS), lambda i: (0, 0)),
            pl.BlockSpec((NROW, 8, BATCH), lambda i: (0, 0, 0)),
        ],
        out_specs=[
            pl.BlockSpec((OUTS, cols), lambda i: (0, i)),
            pl.BlockSpec((OUTS, BATCH), lambda i: (0, 0)),
        ],
        out_shape=[
            jax.ShapeDtypeStruct((OUTS, PDEV), F32),
            jax.ShapeDtypeStruct((OUTS, BATCH), F32),
        ],
        compiler_params=params(),
        cost_estimate=cost(6e9, 2 * MIB, PDEV * BATCH),
        name="direct_part",
    )(row, cent_t, batch_rows, resid)


def step_kernel(core_ref, own_ref, other_ref, direct_ref, *refs):
    his, los = refs[0 : 2 * PARTS : 2], refs[1 : 2 * PARTS : 2]
    out_ref, corr, parts = refs[2 * PARTS :]

    @pl.when(pl.program_id(0) == 0)
    def _():
        place_tiles(core_ref, own_ref, other_ref, corr)
        hi, lo = split2(corr[...])
        parts[:OUTS] = hi
        parts[OUTS:] = lo

    count = NYS // PARTS
    back = jnp.zeros(out_ref.shape, F32)
    for i in range(PARTS):
        at = slice(i * count, (i + 1) * count)
        both = dot(parts[:, at], his[i][...])
        back += both[:OUTS] + both[OUTS:] + dot(parts[:OUTS, at], los[i][...])
    out_ref[...] = RATE * (direct_ref[...] - back)


def step_of(core, own, other, matrices, direct):
    cols = 256
    whole = pl.BlockSpec((NCHIPS, 8, 128), lambda i: (0, 0, 0))
    matrix = pl.BlockSpec((NYS // PARTS, cols), lambda i: (0, i))
    return pl.pallas_call(
        step_kernel,
        grid=(PDEV // cols,),
        in_specs=[
            pl.BlockSpec(memory_space=pltpu.SMEM),
            whole,
            whole,
            pl.BlockSpec((OUTS, cols), lambda i: (0, i)),
        ]
        + [matrix] * (2 * PARTS),
        out_specs=pl.BlockSpec((OUTS, cols), lambda i: (0, i)),
        out_shape=jax.ShapeDtypeStruct((OUTS, PDEV), F32),
        scratch_shapes=[pltpu.VMEM((OUTS, NYS), F32), pltpu.VMEM((2 * OUTS, NYS), BF16)],
        compiler_params=params(56),
        cost_estimate=cost(1.2e10, 36 * MIB),
        name="step_of",
    )(core, own, other, direct, *matrices)


def swap(parts, axes):
    return lax.all_to_all(parts, axes, 0, 0, tiled=True)


def other_core(block):
    return lax.ppermute(block, "core", [(0, 1), (1, 0)])


def over_row(block):
    held = block[None]
    for axis, size, flip in (("core", NCORE, 1), ("x", NX, 1), ("x", NX, 2)):
        moved = lax.ppermute(held, axis, [(i, i ^ flip) for i in range(size)])
        held = jnp.concatenate([held, moved], axis=0)
    return held


def after(value, *first):
    return lax.optimization_barrier((value,) + first)[0]


def finish(core, row, cent_t, wts_t, targets, scale, batch_t, batch_rows, get_nys, eig):
    pred = batch_products(cent_t, batch_rows, wts_t)
    pred = pred.reshape(NROW, 8, BATCH)
    nys = get_nys(pred)
    pred = add_spread(after(swap(pred, ROW), nys), NCOL)

    modes = mode_products(batch_t, after(nys, pred), eig, scale)
    targ = lax.dynamic_slice_in_dim(targets.T, row[0] * 8, 8, 0)
    resid, tiles = correct(after(swap(pred, COL), modes), targ, modes, eig)

    one = nys_parts(cent_t, after(nys, tiles), 0)
    tiles = add_spread(after(swap(tiles, COL), *one), NCHIPS)

    two = nys_parts(cent_t, after(nys, tiles), 1)
    direct, resid_t = direct_part(row, cent_t, batch_rows, over_row(after(resid, tiles)))
    own = after(swap(tiles, CHIPS), direct, *two)
    step_t = step_of(core, own, other_core(own), one + two, direct)
    return resid_t.T, step_t.T


def slotted(centres, weights, targets, batch_index, nystrom_index, eigvecs, mode_scale):
    core = jnp.full((1,), lax.axis_index("core"), jnp.int32)
    row = jnp.full((1,), lax.axis_index(ROW), jnp.int32)
    chip = jnp.full((1,), lax.axis_index(CHIPS), jnp.int32)
    cent_t = centres.T

    index = jnp.concatenate([nystrom_index, batch_index]).reshape(-1, 128)
    keep, send = pack(core, chip, index, cent_t)
    message = join_spread(keep, other_core(send))

    batch_row, nys_row = batch_index[None, :], after(nystrom_index, message)[None, :]
    slots = batch_slots(core, batch_row, nys_row)
    chips = jnp.arange(NCHIPS, dtype=jnp.int32)[:, None]
    starts = jnp.sum((chip_of(nys_row) < chips).astype(jnp.int32), axis=1)
    eig = reorder(row, order(nys_row), over_row(eigvecs.T))

    own = after(swap(message, CHIPS), slots, starts, eig)
    other = other_core(own)
    batch_t, batch_rows = unpack_batch(slots, own, other)
    return finish(
        core,
        row,
        cent_t,
        weights.T,
        targets,
        mode_scale[:, None],
        batch_t,
        batch_rows,
        lambda pred: unpack_nys(core, starts, after(own, pred), other),
        eig,
    )


def select_kernel(index_ref, cent_ref, out_ref):
    hi, mid, low = split3(cent_ref[...])
    parts = jnp.concatenate([hi, mid, low], axis=0).astype(BF16)
    place = lax.broadcasted_iota(jnp.int32, (PDEV, out_ref.shape[1]), 0)
    found = dot(parts, jnp.where(place == index_ref[...], 1.0, 0.0).astype(BF16))
    out_ref[...] = found[:FEATS] + found[FEATS : 2 * FEATS] + found[2 * FEATS :]


def select(index, cent_t):
    n = index.shape[1]
    block = 512
    return pl.pallas_call(
        select_kernel,
        grid=(n // block,),
        in_specs=[
            pl.BlockSpec((1, block), lambda i: (0, i)),
            pl.BlockSpec((FEATS, PDEV), lambda i: (0, 0)),
        ],
        out_specs=pl.BlockSpec((FEATS, block), lambda i: (0, i)),
        out_shape=jax.ShapeDtypeStruct((FEATS, n), F32),
        compiler_params=params(),
        cost_estimate=cost(2 * 192 * PDEV * n, PDEV * 256 + n * 256),
        name="select",
    )(index, cent_t)


def gather_rows(index, cent_t):
    n = index.shape[0]
    offset = lax.axis_index(ALL) * PDEV
    feats = swap(select((index - offset)[None, :], cent_t).reshape(NROW, 8, n), ROW)
    feats = jnp.sum(feats, axis=0).reshape(8, NCOL, n // NCOL).swapaxes(0, 1)
    feats = jnp.sum(swap(feats, COL), axis=0)
    feats = swap(jnp.broadcast_to(feats[None], (NCOL, 8, n // NCOL)), COL)
    feats = feats.swapaxes(0, 1).reshape(8, n)
    return swap(jnp.broadcast_to(feats[None], (NROW, 8, n)), ROW).reshape(FEATS, n)


def general(centres, weights, targets, batch_index, nystrom_index, eigvecs, mode_scale):
    core = jnp.full((1,), lax.axis_index("core"), jnp.int32)
    row = jnp.full((1,), lax.axis_index(ROW), jnp.int32)
    cent_t = centres.T
    batch_t = gather_rows(batch_index, cent_t)
    nys = jnp.pad(gather_rows(nystrom_index, cent_t).T, ((0, SLOTS), (0, 0)))
    eig = reorder(row, jnp.arange(NYS, dtype=jnp.int32)[None, :], over_row(eigvecs.T))
    return finish(
        core,
        row,
        cent_t,
        weights.T,
        targets,
        mode_scale[:, None],
        batch_t,
        batch_t.T,
        lambda pred: nys,
        eig,
    )


def local(*args):
    index = jnp.concatenate([args[3], args[4]])
    chips = jnp.arange(NCHIPS, dtype=jnp.int32)[:, None]
    owned = jnp.sum((chip_of(index)[None, :] == chips).astype(jnp.int32), axis=1)
    fits = jnp.max(owned) <= SLOTS
    result = slotted(*args)
    return lax.cond(fits, lambda done: done, lambda done: general(*args), result)


def solution(mesh):
    fine = Mesh(mesh.devices.reshape(NX, NCORE, 8, 4), ALL)
    in_specs = (
        P(ALL, None),
        P(ALL, None),
        P(),
        P(),
        P(),
        P(ROW, COL),
        P(COL),
    )
    out_specs = (P(), P(ALL, None))
    return jax.shard_map(local, mesh=fine, in_specs=in_specs, out_specs=out_specs, check_vma=False)
```

```python
import functools

import jax
import jax.numpy as jnp
from jax import lax
from jax.experimental import pallas as pl
from jax.experimental.pallas import tpu as pltpu
from jax.sharding import Mesh
from jax.sharding import PartitionSpec as P

F32 = jnp.float32
BF16 = jnp.bfloat16
ROW = ("x", "core")
COL = ("z", "y")
CHIPS = ("x", "z", "y")
ALL = ("x", "core", "z", "y")
NX, NCORE, NROW, NCOL, NCHIPS = 4, 2, 8, 32, 128
FEATS, OUTS, BATCH, NYS, MODES = 64, 64, 512, 4096, 32
PDEV = 2048
SHIFT = 11
SLOTS, SLOTROWS = 64, 16
PARTS = 2
RATE = 0.25
LOG2E = 1.4426950408889634
DEPTH = 6 * FEATS + 128
MIB = 1024 * 1024


def params(mib=24, grid=1):
    return pltpu.CompilerParams(
        vmem_limit_bytes=mib * MIB, dimension_semantics=("arbitrary",) * grid
    )


def cost(flops, nbytes, trans=0):
    return pl.CostEstimate(flops=int(flops), bytes_accessed=int(nbytes), transcendentals=int(trans))


def dot(a, b):
    return lax.dot_general(a, b, (((1,), (0,)), ((), ())), preferred_element_type=F32)


def dot_nt(a, b):
    return lax.dot_general(a, b, (((1,), (1,)), ((), ())), preferred_element_type=F32)


def split2(v):
    hi = v.astype(BF16)
    lo = (v - hi.astype(F32)).astype(BF16)
    return hi, lo


def split3(v):
    hi = v.astype(BF16).astype(F32)
    rest = v - hi
    mid = rest.astype(BF16).astype(F32)
    low = (rest - mid).astype(BF16).astype(F32)
    return hi, mid, low


def left_side(a):
    ah, am, al = split3(a * (2.0 * LOG2E / FEATS))
    sq = split3(jnp.sum(a * a, axis=1, keepdims=True) * (-LOG2E / FEATS))
    lane = lax.broadcasted_iota(jnp.int32, (a.shape[0], 128), 1)
    extra = jnp.where((lane >= 3) & (lane < 6), 1.0, 0.0)
    for i in range(3):
        extra = jnp.where(lane == i, sq[i], extra)
    return jnp.concatenate([ah, ah, am, am, ah, al, extra], axis=1).astype(BF16)


def right_side(bt):
    bh, bm, bl = split3(bt)
    sq = split3(jnp.sum(bt * bt, axis=0, keepdims=True) * (-LOG2E / FEATS))
    row = lax.broadcasted_iota(jnp.int32, (128, bt.shape[1]), 0)
    extra = jnp.where(row < 3, 1.0, 0.0)
    for i in range(3):
        extra = jnp.where(row == 3 + i, sq[i], extra)
    return jnp.concatenate([bh, bm, bh, bm, bl, bh, extra], axis=0).astype(BF16)


def kern(left, right):
    return jnp.exp2(dot(left, right))


def chip_of(index):
    owner = lax.shift_right_logical(index, SHIFT)
    return lax.shift_right_logical(owner, 6) * NCOL + (owner & (NCOL - 1))


def core_of(index):
    return lax.shift_right_logical(index, SHIFT + 5) & 1


def pack_kernel(core_ref, chip_ref, index_ref, cent_ref, keep_ref, send_ref):
    rows = index_ref.shape[0]
    index = index_ref[...]
    ours = chip_of(index) == chip_ref[0]
    ones = jnp.where(ours, 1.0, 0.0).astype(BF16)
    lane_from = lax.broadcasted_iota(jnp.int32, (128, 128), 0)
    lane_to = lax.broadcasted_iota(jnp.int32, (128, 128), 1)
    in_row = dot(ones, jnp.where(lane_from < lane_to, 1.0, 0.0).astype(BF16))
    row_to = lax.broadcasted_iota(jnp.int32, (rows, rows), 0)
    row_from = lax.broadcasted_iota(jnp.int32, (rows, rows), 1)
    before = dot(jnp.where(row_from < row_to, 1.0, 0.0).astype(BF16), ones)
    rank = in_row + jnp.sum(before, axis=1, keepdims=True)
    rank = jnp.where(ours & (core_of(index) == core_ref[0]), rank, -1.0)
    local_row = (index & (PDEV - 1)).astype(F32) + 1.0

    slot = lax.broadcasted_iota(jnp.int32, (SLOTS, 128), 0).astype(F32)
    found = jnp.zeros((SLOTS, 128), F32)
    for i in range(rows):
        found += jnp.where(rank[i : i + 1] == slot, local_row[i : i + 1], 0.0)
    source = jnp.sum(found, axis=1, keepdims=True).astype(jnp.int32) - 1
    place = lax.broadcasted_iota(jnp.int32, (SLOTS, PDEV), 1)
    chosen = jnp.where(place == source, 1.0, 0.0).astype(BF16)
    hi, mid, low = split3(cent_ref[...])
    parts = jnp.concatenate([hi, mid, low], axis=0).astype(BF16)
    got = dot_nt(chosen, parts)
    got = got[:, :FEATS] + got[:, FEATS : 2 * FEATS] + got[:, 2 * FEATS :]
    n = SLOTROWS
    zero = jnp.concatenate([got[:n], got[n : 2 * n]], axis=1)
    one = jnp.concatenate([got[2 * n : 3 * n], got[3 * n :]], axis=1)
    at_zero = core_ref[0] == 0
    keep_ref[...] = jnp.where(at_zero, zero, one)
    send_ref[...] = jnp.where(at_zero, one, zero)


def pack(core, chip, index, cent_t):
    smem = pl.BlockSpec(memory_space=pltpu.SMEM)
    vmem = pl.BlockSpec(memory_space=pltpu.VMEM)
    shape = jax.ShapeDtypeStruct((SLOTROWS, 128), F32)
    return pl.pallas_call(
        pack_kernel,
        in_specs=[smem, smem, vmem, vmem],
        out_shape=[shape, shape],
        compiler_params=params(grid=0),
        cost_estimate=cost(1e9, 2 * MIB),
        name="pack",
    )(core, chip, index, cent_t)


def join_spread_kernel(keep_ref, came_ref, out_ref):
    message = keep_ref[...] + came_ref[...]
    for i in range(out_ref.shape[0]):
        out_ref[i] = message


def join_spread(keep, came):
    return pl.pallas_call(
        join_spread_kernel,
        out_shape=jax.ShapeDtypeStruct((NCHIPS,) + keep.shape, F32),
        compiler_params=params(grid=0),
        cost_estimate=cost(0, MIB),
        name="join_spread",
    )(keep, came)


def across_rows(row):
    return jnp.broadcast_to(row.astype(F32), (128, row.shape[1])).T


def batch_slots_kernel(core_ref, batch_ref, nys_ref, out_ref):
    index = batch_ref[...]
    chip = chip_of(index)
    source = lax.broadcasted_iota(jnp.int32, (BATCH, 128), 0)
    lane = lax.broadcasted_iota(jnp.int32, (BATCH, 128), 1)
    from_batch = across_rows(chip)
    from_nys = across_rows(chip_of(nys_ref[...]))
    for k in range(BATCH // 128):
        here = chip[:, k * 128 : (k + 1) * 128]
        target = here.astype(F32)
        ahead = (from_batch == target) & (source < lane + k * 128)
        rank = jnp.sum(jnp.where(ahead, 1.0, 0.0), axis=0, keepdims=True)
        rank += jnp.sum(jnp.where(from_nys == target, 1.0, 0.0), axis=0, keepdims=True)
        rank = rank.astype(jnp.int32)
        place = here * SLOTROWS + (rank & (SLOTROWS - 1))
        piece = lax.shift_right_logical(rank, 4)
        for which in range(2):
            core = core_ref[0] if which == 0 else 1 - core_ref[0]
            for half in range(2):
                at = 2 * which + half
                value = jnp.where(piece == 2 * core + half, place, -1)
                out_ref[at : at + 1, k * 128 : (k + 1) * 128] = value


def batch_slots(core, batch_index, nys_index):
    vmem = pl.BlockSpec(memory_space=pltpu.VMEM)
    return pl.pallas_call(
        batch_slots_kernel,
        in_specs=[pl.BlockSpec(memory_space=pltpu.SMEM), vmem, vmem],
        out_shape=jax.ShapeDtypeStruct((4, BATCH), jnp.int32),
        compiler_params=params(grid=0),
        cost_estimate=cost(1e6, MIB),
        name="batch_slots",
    )(core, batch_index, nys_index)


def unpack_batch_kernel(slot_ref, own_ref, other_ref, out_ref):
    chips = 64
    rows = chips * SLOTROWS
    total = jnp.zeros((3 * FEATS, BATCH), F32)
    for which, ref in ((0, own_ref), (1, other_ref)):
        for part in range(NCHIPS // chips):
            block = ref[part * chips : (part + 1) * chips].reshape(rows, 128).T
            hi, mid, low = split3(block)
            place = lax.broadcasted_iota(jnp.int32, (rows, BATCH), 0) + part * rows
            for half in range(2):
                at = slice(half * FEATS, (half + 1) * FEATS)
                parts = jnp.concatenate([hi[at], mid[at], low[at]], axis=0).astype(BF16)
                slot = slot_ref[2 * which + half : 2 * which + half + 1]
                total += dot(parts, jnp.where(place == slot, 1.0, 0.0).astype(BF16))
    feats = total[:FEATS] + total[FEATS : 2 * FEATS] + total[2 * FEATS :]
    out_ref[...] = feats.T


def unpack_batch(slots, own, other):
    return pl.pallas_call(
        unpack_batch_kernel,
        out_shape=jax.ShapeDtypeStruct((BATCH, FEATS), F32),
        compiler_params=params(grid=0),
        cost_estimate=cost(1e9, 4 * MIB),
        name="unpack_batch",
    )(slots, own, other)


def unpack_nys_kernel(core_ref, start_ref, own_ref, other_ref, out_ref, held):
    n = SLOTROWS

    def run(zero_ref, one_ref):
        def body(i, _):
            at = start_ref[i]
            zero, one = zero_ref[i], one_ref[i]
            held[pl.ds(at, n), :] = zero[:, :FEATS]
            held[pl.ds(at + n, n), :] = zero[:, FEATS:]
            held[pl.ds(at + 2 * n, n), :] = one[:, :FEATS]
            held[pl.ds(at + 3 * n, n), :] = one[:, FEATS:]
            return 0

        lax.fori_loop(0, NCHIPS, body, 0, unroll=8)

    @pl.when(core_ref[0] == 0)
    def _():
        run(own_ref, other_ref)

    @pl.when(core_ref[0] == 1)
    def _():
        run(other_ref, own_ref)

    out_ref[...] = held[:NYS, :].T


def unpack_nys(core, starts, own, other):
    smem = pl.BlockSpec(memory_space=pltpu.SMEM)
    vmem = pl.BlockSpec(memory_space=pltpu.VMEM)
    return pl.pallas_call(
        unpack_nys_kernel,
        in_specs=[smem, smem, vmem, vmem],
        out_shape=jax.ShapeDtypeStruct((FEATS, NYS), F32),
        scratch_shapes=[pltpu.VMEM((NYS + SLOTS, FEATS), F32)],
        compiler_params=params(grid=0),
        cost_estimate=cost(0, 8 * MIB),
        name="unpack_nys",
    )(core, starts, own, other)


def order_kernel(index_ref, out_ref):
    chip = chip_of(index_ref[...])
    chips = lax.broadcasted_iota(jnp.int32, (NCHIPS, NYS), 0)
    member = jnp.where(chips == chip, 1.0, 0.0)
    lower = lax.broadcasted_iota(jnp.int32, (128, 128), 0)
    upper = lax.broadcasted_iota(jnp.int32, (128, 128), 1)
    counts = jnp.sum(member, axis=1, keepdims=True)
    start = jnp.dot(
        jnp.where(upper < lower, 1.0, 0.0),
        jnp.broadcast_to(counts, (NCHIPS, 128)),
        precision=lax.Precision.HIGHEST,
        preferred_element_type=F32,
    )
    earlier = jnp.where(lower < upper, 1.0, 0.0).astype(BF16)
    for k in range(NYS // 128):
        block = member[:, k * 128 : (k + 1) * 128]
        place = dot(block.astype(BF16), earlier) + start
        place = jnp.sum(block * place, axis=0, keepdims=True)
        out_ref[:, k * 128 : (k + 1) * 128] = place.astype(jnp.int32)
        start = start + jnp.sum(block, axis=1, keepdims=True)


def order(index):
    return pl.pallas_call(
        order_kernel,
        out_shape=jax.ShapeDtypeStruct((1, NYS), jnp.int32),
        compiler_params=params(grid=0),
        cost_estimate=cost(1e9, 4 * MIB),
        name="order",
    )(index)


def reorder_kernel(row_ref, order_ref, eig_ref, out_ref, parts):
    width = out_ref.shape[1]
    step = pl.program_id(0)
    block = NYS // NROW

    @pl.when(step == 0)
    def _():
        for i in range(NROW):
            at = pl.multiple_of((row_ref[0] ^ i) * block, block)
            hi, mid, low = split3(eig_ref[i])
            parts[:, pl.ds(at, block)] = jnp.concatenate([hi, mid, low], axis=0).astype(BF16)

    place = lax.broadcasted_iota(jnp.int32, (width, NYS), 0) + step * width
    chosen = jnp.where(place == order_ref[...], 1.0, 0.0).astype(BF16)
    got = dot_nt(parts[...], chosen)
    out_ref[...] = got[:MODES] + got[MODES : 2 * MODES] + got[2 * MODES :]


def reorder(row, orders, eig):
    block = 512
    return pl.pallas_call(
        reorder_kernel,
        grid=(NYS // block,),
        in_specs=[
            pl.BlockSpec(memory_space=pltpu.SMEM),
            pl.BlockSpec((1, NYS), lambda i: (0, 0)),
            pl.BlockSpec((NROW, MODES, NYS // NROW), lambda i: (0, 0, 0)),
        ],
        out_specs=pl.BlockSpec((MODES, block), lambda i: (0, i)),
        out_shape=jax.ShapeDtypeStruct((MODES, NYS), F32),
        scratch_shapes=[pltpu.VMEM((3 * MODES, NYS), BF16)],
        compiler_params=params(),
        cost_estimate=cost(1e10, 2 * MIB),
        name="reorder",
    )(row, orders, eig)


def add_spread_kernel(in_ref, out_ref):
    total = in_ref[0]
    for i in range(1, in_ref.shape[0]):
        total = total + in_ref[i]
    for i in range(out_ref.shape[0]):
        out_ref[i] = total


def add_spread(parts, copies):
    return pl.pallas_call(
        add_spread_kernel,
        out_shape=jax.ShapeDtypeStruct((copies,) + parts.shape[1:], F32),
        compiler_params=params(grid=0),
        cost_estimate=cost(parts.size, parts.size * 4 + parts.size // parts.shape[0] * copies * 4),
        name="add_spread",
    )(parts)


def place_tiles(core_ref, own_ref, other_ref, out_ref):
    mine = core_ref[0]
    for x in range(NX):
        for part, core in ((own_ref, mine), (other_ref, 1 - mine)):
            at = pl.multiple_of((2 * x + core) * 8, 8)
            for c in range(NCOL):
                out_ref[pl.ds(at, 8), c * 128 : (c + 1) * 128] = part[x * NCOL + c]


def batch_kernel(cent_ref, batch_ref, wts_ref, pred_ref, left):
    @pl.when(pl.program_id(0) == 0)
    def _():
        left[...] = left_side(batch_ref[...])

    khi, klo = split2(kern(left[...], right_side(cent_ref[...])))
    whi, wlo = split2(wts_ref[...])
    both = dot_nt(jnp.concatenate([whi, wlo], axis=0), khi)
    part = both[:OUTS] + both[OUTS:] + dot_nt(whi, klo)

    @pl.when(pl.program_id(0) == 0)
    def _():
        pred_ref[...] = part

    @pl.when(pl.program_id(0) > 0)
    def _():
        pred_ref[...] += part


def batch_products(cent_t, batch_rows, wts_t):
    cols = 512
    return pl.pallas_call(
        batch_kernel,
        grid=(PDEV // cols,),
        in_specs=[
            pl.BlockSpec((FEATS, cols), lambda i: (0, i)),
            pl.BlockSpec((BATCH, FEATS), lambda i: (0, 0)),
            pl.BlockSpec((OUTS, cols), lambda i: (0, i)),
        ],
        out_specs=pl.BlockSpec((OUTS, BATCH), lambda i: (0, 0)),
        out_shape=jax.ShapeDtypeStruct((OUTS, BATCH), F32),
        scratch_shapes=[pltpu.VMEM((BATCH, DEPTH), BF16)],
        compiler_params=params(),
        cost_estimate=cost(6e9, 2 * MIB, PDEV * BATCH),
        name="batch_products",
    )(cent_t, batch_rows, wts_t)


def modes_kernel(batch_ref, nys_ref, eig_ref, scale_ref, out_ref, left):
    step = pl.program_id(0)

    @pl.when(step == 0)
    def _():
        left[...] = left_side(batch_ref[...])

    khi, klo = split2(kern(left[...], right_side(nys_ref[...])))
    ehi, elo = split2(eig_ref[...])
    both = dot_nt(jnp.concatenate([ehi, elo], axis=0), khi)
    part = both[:MODES] + both[MODES:] + dot_nt(ehi, klo)

    @pl.when(step == 0)
    def _():
        out_ref[...] = part

    @pl.when(step > 0)
    def _():
        out_ref[...] += part

    @pl.when(step == pl.num_programs(0) - 1)
    def _():
        out_ref[...] = out_ref[...] * scale_ref[...]


def mode_products(batch_rows, nys_t, eig, scale):
    block = 512
    return pl.pallas_call(
        modes_kernel,
        grid=(NYS // block,),
        in_specs=[
            pl.BlockSpec((BATCH, FEATS), lambda i: (0, 0)),
            pl.BlockSpec((FEATS, block), lambda i: (0, i)),
            pl.BlockSpec((MODES, block), lambda i: (0, i)),
            pl.BlockSpec((MODES, 1), lambda i: (0, 0)),
        ],
        out_specs=pl.BlockSpec((MODES, BATCH), lambda i: (0, 0)),
        out_shape=jax.ShapeDtypeStruct((MODES, BATCH), F32),
        scratch_shapes=[pltpu.VMEM((BATCH, DEPTH), BF16)],
        compiler_params=params(),
        cost_estimate=cost(1e10, 3 * MIB, NYS * BATCH),
        name="mode_products",
    )(batch_rows, nys_t, eig, scale)


def nys_kernel(cent_ref, nys_ref, hi_ref, lo_ref, left):
    @pl.when(pl.program_id(0) == 0)
    def _():
        left[...] = left_side(cent_ref[...].T)

    khi, klo = split2(kern(left[...], right_side(nys_ref[...])))
    hi_ref[...] = khi
    lo_ref[...] = klo


def nys_parts(cent_t, nys_t, part):
    block = 256
    count = NYS // PARTS
    shape = jax.ShapeDtypeStruct((PDEV, count), BF16)
    return pl.pallas_call(
        nys_kernel,
        grid=(count // block,),
        in_specs=[
            pl.BlockSpec((FEATS, PDEV), lambda j: (0, 0)),
            pl.BlockSpec((FEATS, block), lambda j: (0, j + part * (count // block))),
        ],
        out_specs=[pl.BlockSpec((PDEV, block), lambda j: (0, j))] * 2,
        out_shape=[shape, shape],
        scratch_shapes=[pltpu.VMEM((PDEV, DEPTH), BF16)],
        compiler_params=params(56),
        cost_estimate=cost(1.8e10 / PARTS, 34 * MIB / PARTS, PDEV * NYS / PARTS),
        name="nys_parts",
    )(cent_t, nys_t)


def correct_kernel(pred_ref, targ_ref, modes_ref, eig_ref, resid_ref, tiles_ref):
    total = pred_ref[0]
    for i in range(1, NCOL):
        total = total + pred_ref[i]
    resid = total - targ_ref[...]
    resid_ref[...] = resid
    coeff = lax.dot_general(
        resid,
        modes_ref[...],
        (((1,), (1,)), ((), ())),
        precision=lax.Precision.HIGHEST,
        preferred_element_type=F32,
    )
    share = jnp.dot(
        coeff, eig_ref[...], precision=lax.Precision.HIGHEST, preferred_element_type=F32
    )
    for k in range(NCOL):
        tiles_ref[k] = share[:, k * 128 : (k + 1) * 128]


def correct(pred, targ, modes, eig):
    return pl.pallas_call(
        correct_kernel,
        out_shape=[
            jax.ShapeDtypeStruct((8, BATCH), F32),
            jax.ShapeDtypeStruct((NCOL, 8, 128), F32),
        ],
        compiler_params=params(grid=0),
        cost_estimate=cost(1e8, 2 * MIB),
        name="correct",
    )(pred, targ, modes, eig)


def direct_kernel(row_ref, cent_ref, batch_ref, resid_ref, out_ref, outr_ref, left):
    @pl.when(pl.program_id(0) == 0)
    def _():
        left[...] = left_side(batch_ref[...])
        for i in range(NROW):
            at = pl.multiple_of((row_ref[0] ^ i) * 8, 8)
            outr_ref[pl.ds(at, 8), :] = resid_ref[i]

    khi, klo = split2(kern(left[...], right_side(cent_ref[...])))
    rhi, rlo = split2(outr_ref[...])
    both = dot(jnp.concatenate([rhi, rlo], axis=0), khi)
    out_ref[...] = both[:OUTS] + both[OUTS:] + dot(rhi, klo)


def direct_part(row, cent_t, batch_rows, resid):
    cols = 512
    return pl.pallas_call(
        direct_kernel,
        grid=(PDEV // cols,),
        in_specs=[
            pl.BlockSpec(memory_space=pltpu.SMEM),
            pl.BlockSpec((FEATS, cols), lambda i: (0, i)),
            pl.BlockSpec((BATCH, FEATS), lambda i: (0, 0)),
            pl.BlockSpec((NROW, 8, BATCH), lambda i: (0, 0, 0)),
        ],
        out_specs=[
            pl.BlockSpec((OUTS, cols), lambda i: (0, i)),
            pl.BlockSpec((OUTS, BATCH), lambda i: (0, 0)),
        ],
        out_shape=[
            jax.ShapeDtypeStruct((OUTS, PDEV), F32),
            jax.ShapeDtypeStruct((OUTS, BATCH), F32),
        ],
        scratch_shapes=[pltpu.VMEM((BATCH, DEPTH), BF16)],
        compiler_params=params(),
        cost_estimate=cost(6e9, 2 * MIB, PDEV * BATCH),
        name="direct_part",
    )(row, cent_t, batch_rows, resid)


def step_kernel(core_ref, own_ref, other_ref, direct_ref, *refs):
    his, los = refs[0 : 2 * PARTS : 2], refs[1 : 2 * PARTS : 2]
    out_ref, corr, parts, total = refs[2 * PARTS :]
    step = pl.program_id(0)
    width = his[0].shape[1]

    @pl.when(step == 0)
    def _():
        place_tiles(core_ref, own_ref, other_ref, corr)
        hi = corr[...].astype(BF16).astype(F32)
        parts[...] = jnp.concatenate([hi, corr[...] - hi], axis=0).T.astype(BF16)

    more = jnp.zeros((PDEV, 2 * OUTS), F32)
    for i in range(PARTS):
        at = pl.multiple_of(i * (NYS // PARTS) + step * width, width)
        coeff = parts[pl.ds(at, width), :]
        more += dot(his[i][...], coeff) + dot(los[i][...], coeff)

    @pl.when(step == 0)
    def _():
        total[...] = more

    @pl.when(step > 0)
    def _():
        total[...] += more

    @pl.when(step == pl.num_programs(0) - 1)
    def _():
        back = total[...].T
        out_ref[...] = RATE * (direct_ref[...] - (back[:OUTS] + back[OUTS:]))


def step_of(core, own, other, matrices, direct):
    width = 256
    whole = pl.BlockSpec((NCHIPS, 8, 128), lambda i: (0, 0, 0))
    matrix = pl.BlockSpec((PDEV, width), lambda i: (0, i))
    return pl.pallas_call(
        step_kernel,
        grid=(NYS // PARTS // width,),
        in_specs=[
            pl.BlockSpec(memory_space=pltpu.SMEM),
            whole,
            whole,
            pl.BlockSpec((OUTS, PDEV), lambda i: (0, 0)),
        ]
        + [matrix] * (2 * PARTS),
        out_specs=pl.BlockSpec((OUTS, PDEV), lambda i: (0, 0)),
        out_shape=jax.ShapeDtypeStruct((OUTS, PDEV), F32),
        scratch_shapes=[
            pltpu.VMEM((OUTS, NYS), F32),
            pltpu.VMEM((NYS, 2 * OUTS), BF16),
            pltpu.VMEM((PDEV, 2 * OUTS), F32),
        ],
        compiler_params=params(56),
        cost_estimate=cost(1.2e10, 36 * MIB),
        name="step_of",
    )(core, own, other, direct, *matrices)


def swap(parts, axes):
    return lax.all_to_all(parts, axes, 0, 0, tiled=True)


def other_core(block):
    return lax.ppermute(block, "core", [(0, 1), (1, 0)])


def over_row(block):
    held = block[None]
    for axis, size, flip in (("core", NCORE, 1), ("x", NX, 1), ("x", NX, 2)):
        moved = lax.ppermute(held, axis, [(i, i ^ flip) for i in range(size)])
        held = jnp.concatenate([held, moved], axis=0)
    return held


def after(value, *first):
    return lax.optimization_barrier((value,) + first)[0]


def finish(core, row, cent_t, wts_t, targets, scale, batch_rows, get_nys, eig):
    pred = batch_products(cent_t, batch_rows, wts_t).reshape(NROW, 8, BATCH)
    nys_t = get_nys(pred)
    pred = add_spread(after(swap(pred, ROW), nys_t), NCOL)

    sent = after(nys_t, pred)
    modes = mode_products(batch_rows, sent, eig, scale)
    one = nys_parts(cent_t, sent, 0)
    targ = lax.dynamic_slice_in_dim(targets.T, row[0] * 8, 8, 0)
    resid, tiles = correct(after(swap(pred, COL), modes, *one), targ, modes, eig)

    two = nys_parts(cent_t, after(nys_t, tiles), 1)
    tiles = add_spread(after(swap(tiles, COL), *two), NCHIPS)

    direct, resid_t = direct_part(row, cent_t, batch_rows, over_row(after(resid, tiles)))
    own = after(swap(tiles, CHIPS), direct)
    step_t = step_of(core, own, other_core(own), one + two, direct)
    return resid_t.T, step_t.T


def slotted(centres, weights, targets, batch_index, nystrom_index, eigvecs, mode_scale):
    core = jnp.full((1,), lax.axis_index("core"), jnp.int32)
    row = jnp.full((1,), lax.axis_index(ROW), jnp.int32)
    chip = jnp.full((1,), lax.axis_index(CHIPS), jnp.int32)
    cent_t = centres.T

    index = jnp.concatenate([nystrom_index, batch_index]).reshape(-1, 128)
    keep, send = pack(core, chip, index, cent_t)
    message = join_spread(keep, other_core(send))

    batch_row, nys_row = batch_index[None, :], after(nystrom_index, message)[None, :]
    slots = batch_slots(core, batch_row, nys_row)
    chips = jnp.arange(NCHIPS, dtype=jnp.int32)[:, None]
    starts = jnp.sum((chip_of(nys_row) < chips).astype(jnp.int32), axis=1)
    eig = reorder(row, order(nys_row), over_row(eigvecs.T))

    own = after(swap(message, CHIPS), slots, starts, eig)
    other = other_core(own)
    batch_rows = unpack_batch(slots, own, other)
    return finish(
        core,
        row,
        cent_t,
        weights.T,
        targets,
        mode_scale[:, None],
        batch_rows,
        lambda pred: unpack_nys(core, starts, after(own, pred), other),
        eig,
    )


def select_kernel(index_ref, cent_ref, out_ref):
    hi, mid, low = split3(cent_ref[...])
    parts = jnp.concatenate([hi, mid, low], axis=0).astype(BF16)
    place = lax.broadcasted_iota(jnp.int32, (PDEV, out_ref.shape[1]), 0)
    found = dot(parts, jnp.where(place == index_ref[...], 1.0, 0.0).astype(BF16))
    out_ref[...] = found[:FEATS] + found[FEATS : 2 * FEATS] + found[2 * FEATS :]


def select(index, cent_t):
    n = index.shape[1]
    block = 512
    return pl.pallas_call(
        select_kernel,
        grid=(n // block,),
        in_specs=[
            pl.BlockSpec((1, block), lambda i: (0, i)),
            pl.BlockSpec((FEATS, PDEV), lambda i: (0, 0)),
        ],
        out_specs=pl.BlockSpec((FEATS, block), lambda i: (0, i)),
        out_shape=jax.ShapeDtypeStruct((FEATS, n), F32),
        compiler_params=params(),
        cost_estimate=cost(2 * 192 * PDEV * n, PDEV * 256 + n * 256),
        name="select",
    )(index, cent_t)


def gather_rows(index, cent_t):
    n = index.shape[0]
    offset = lax.axis_index(ALL) * PDEV
    feats = swap(select((index - offset)[None, :], cent_t).reshape(NROW, 8, n), ROW)
    feats = jnp.sum(feats, axis=0).reshape(8, NCOL, n // NCOL).swapaxes(0, 1)
    feats = jnp.sum(swap(feats, COL), axis=0)
    feats = swap(jnp.broadcast_to(feats[None], (NCOL, 8, n // NCOL)), COL)
    feats = feats.swapaxes(0, 1).reshape(8, n)
    return swap(jnp.broadcast_to(feats[None], (NROW, 8, n)), ROW).reshape(FEATS, n)


def general(centres, weights, targets, batch_index, nystrom_index, eigvecs, mode_scale):
    core = jnp.full((1,), lax.axis_index("core"), jnp.int32)
    row = jnp.full((1,), lax.axis_index(ROW), jnp.int32)
    cent_t = centres.T
    batch_t = gather_rows(batch_index, cent_t)
    nys_t = gather_rows(nystrom_index, cent_t)
    eig = reorder(row, jnp.arange(NYS, dtype=jnp.int32)[None, :], over_row(eigvecs.T))
    return finish(
        core,
        row,
        cent_t,
        weights.T,
        targets,
        mode_scale[:, None],
        batch_t.T,
        lambda pred: nys_t,
        eig,
    )


def local(*args):
    index = jnp.concatenate([args[3], args[4]])
    chips = jnp.arange(NCHIPS, dtype=jnp.int32)[:, None]
    owned = jnp.sum((chip_of(index)[None, :] == chips).astype(jnp.int32), axis=1)
    fits = jnp.max(owned) <= SLOTS
    result = slotted(*args)
    return lax.cond(fits, lambda done: done, lambda done: general(*args), result)


def solution(mesh):
    fine = Mesh(mesh.devices.reshape(NX, NCORE, 8, 4), ALL)
    in_specs = (
        P(ALL, None),
        P(ALL, None),
        P(),
        P(),
        P(),
        P(ROW, COL),
        P(COL),
    )
    out_specs = (P(), P(ALL, None))
    return jax.shard_map(local, mesh=fine, in_specs=in_specs, out_specs=out_specs, check_vma=False)
```

```python
import functools

import jax
import jax.numpy as jnp
from jax import lax
from jax.experimental import pallas as pl
from jax.experimental.pallas import tpu as pltpu
from jax.sharding import Mesh
from jax.sharding import PartitionSpec as P

F32 = jnp.float32
BF16 = jnp.bfloat16
ROW = ("x", "core")
COL = ("z", "y")
CHIPS = ("x", "z", "y")
ALL = ("x", "core", "z", "y")
NX, NCORE, NROW, NCOL, NCHIPS = 4, 2, 8, 32, 128
FEATS, OUTS, BATCH, NYS, MODES = 64, 64, 512, 4096, 32
PDEV = 2048
SHIFT = 11
SLOTS, SLOTROWS = 64, 16
PARTS = 2
RATE = 0.25
LOG2E = 1.4426950408889634
DEPTH = 6 * FEATS + 128
MIB = 1024 * 1024


def params(mib=14, grid=1):
    return pltpu.CompilerParams(
        vmem_limit_bytes=mib * MIB, dimension_semantics=("arbitrary",) * grid
    )


def cost(flops, nbytes, trans=0):
    return pl.CostEstimate(flops=int(flops), bytes_accessed=int(nbytes), transcendentals=int(trans))


def dot(a, b):
    return lax.dot_general(a, b, (((1,), (0,)), ((), ())), preferred_element_type=F32)


def dot_nt(a, b):
    return lax.dot_general(a, b, (((1,), (1,)), ((), ())), preferred_element_type=F32)


def split2(v):
    hi = v.astype(BF16)
    lo = (v - hi.astype(F32)).astype(BF16)
    return hi, lo


def split3(v):
    hi = v.astype(BF16).astype(F32)
    rest = v - hi
    mid = rest.astype(BF16).astype(F32)
    low = (rest - mid).astype(BF16).astype(F32)
    return hi, mid, low


def left_side(a):
    ah, am, al = split3(a * (2.0 * LOG2E / FEATS))
    sq = split3(jnp.sum(a * a, axis=1, keepdims=True) * (-LOG2E / FEATS))
    lane = lax.broadcasted_iota(jnp.int32, (a.shape[0], 128), 1)
    extra = jnp.where((lane >= 3) & (lane < 6), 1.0, 0.0)
    for i in range(3):
        extra = jnp.where(lane == i, sq[i], extra)
    return jnp.concatenate([ah, ah, am, am, ah, al, extra], axis=1).astype(BF16)


def right_side(bt):
    bh, bm, bl = split3(bt)
    sq = split3(jnp.sum(bt * bt, axis=0, keepdims=True) * (-LOG2E / FEATS))
    row = lax.broadcasted_iota(jnp.int32, (128, bt.shape[1]), 0)
    extra = jnp.where(row < 3, 1.0, 0.0)
    for i in range(3):
        extra = jnp.where(row == 3 + i, sq[i], extra)
    return jnp.concatenate([bh, bm, bh, bm, bl, bh, extra], axis=0).astype(BF16)


def kern(left, right):
    return jnp.exp2(dot(left, right))


def chip_of(index):
    owner = lax.shift_right_logical(index, SHIFT)
    return lax.shift_right_logical(owner, 6) * NCOL + (owner & (NCOL - 1))


def core_of(index):
    return lax.shift_right_logical(index, SHIFT + 5) & 1


def pack_kernel(core_ref, chip_ref, index_ref, cent_ref, keep_ref, send_ref):
    rows = index_ref.shape[0]
    index = index_ref[...]
    ours = chip_of(index) == chip_ref[0]
    ones = jnp.where(ours, 1.0, 0.0).astype(BF16)
    lane_from = lax.broadcasted_iota(jnp.int32, (128, 128), 0)
    lane_to = lax.broadcasted_iota(jnp.int32, (128, 128), 1)
    in_row = dot(ones, jnp.where(lane_from < lane_to, 1.0, 0.0).astype(BF16))
    row_to = lax.broadcasted_iota(jnp.int32, (rows, rows), 0)
    row_from = lax.broadcasted_iota(jnp.int32, (rows, rows), 1)
    before = dot(jnp.where(row_from < row_to, 1.0, 0.0).astype(BF16), ones)
    rank = in_row + jnp.sum(before, axis=1, keepdims=True)
    rank = jnp.where(ours & (core_of(index) == core_ref[0]), rank, -1.0)
    local_row = (index & (PDEV - 1)).astype(F32) + 1.0

    slot = lax.broadcasted_iota(jnp.int32, (SLOTS, 128), 0).astype(F32)
    found = jnp.zeros((SLOTS, 128), F32)
    for i in range(rows):
        found += jnp.where(rank[i : i + 1] == slot, local_row[i : i + 1], 0.0)
    source = jnp.sum(found, axis=1, keepdims=True).astype(jnp.int32) - 1
    place = lax.broadcasted_iota(jnp.int32, (SLOTS, PDEV), 1)
    chosen = jnp.where(place == source, 1.0, 0.0).astype(BF16)
    hi, mid, low = split3(cent_ref[...])
    parts = jnp.concatenate([hi, mid, low], axis=0).astype(BF16)
    got = dot_nt(chosen, parts)
    got = got[:, :FEATS] + got[:, FEATS : 2 * FEATS] + got[:, 2 * FEATS :]
    n = SLOTROWS
    zero = jnp.concatenate([got[:n], got[n : 2 * n]], axis=1)
    one = jnp.concatenate([got[2 * n : 3 * n], got[3 * n :]], axis=1)
    at_zero = core_ref[0] == 0
    keep_ref[...] = jnp.where(at_zero, zero, one)
    send_ref[...] = jnp.where(at_zero, one, zero)


def pack(core, chip, index, cent_t):
    smem = pl.BlockSpec(memory_space=pltpu.SMEM)
    vmem = pl.BlockSpec(memory_space=pltpu.VMEM)
    shape = jax.ShapeDtypeStruct((SLOTROWS, 128), F32)
    return pl.pallas_call(
        pack_kernel,
        in_specs=[smem, smem, vmem, vmem],
        out_shape=[shape, shape],
        compiler_params=params(grid=0),
        cost_estimate=cost(1e9, 2 * MIB),
        name="pack",
    )(core, chip, index, cent_t)


def join_spread_kernel(keep_ref, came_ref, out_ref):
    message = keep_ref[...] + came_ref[...]
    for i in range(out_ref.shape[0]):
        out_ref[i] = message


def join_spread(keep, came):
    return pl.pallas_call(
        join_spread_kernel,
        out_shape=jax.ShapeDtypeStruct((NCHIPS,) + keep.shape, F32),
        compiler_params=params(grid=0),
        cost_estimate=cost(0, MIB),
        name="join_spread",
    )(keep, came)


def across_rows(row):
    return jnp.broadcast_to(row.astype(F32), (128, row.shape[1])).T


def batch_slots_kernel(core_ref, batch_ref, nys_ref, out_ref):
    index = batch_ref[...]
    chip = chip_of(index)
    source = lax.broadcasted_iota(jnp.int32, (BATCH, 128), 0)
    lane = lax.broadcasted_iota(jnp.int32, (BATCH, 128), 1)
    from_batch = across_rows(chip)
    from_nys = across_rows(chip_of(nys_ref[...]))
    for k in range(BATCH // 128):
        here = chip[:, k * 128 : (k + 1) * 128]
        target = here.astype(F32)
        ahead = (from_batch == target) & (source < lane + k * 128)
        rank = jnp.sum(jnp.where(ahead, 1.0, 0.0), axis=0, keepdims=True)
        rank += jnp.sum(jnp.where(from_nys == target, 1.0, 0.0), axis=0, keepdims=True)
        rank = rank.astype(jnp.int32)
        place = here * SLOTROWS + (rank & (SLOTROWS - 1))
        piece = lax.shift_right_logical(rank, 4)
        for which in range(2):
            core = core_ref[0] if which == 0 else 1 - core_ref[0]
            for half in range(2):
                at = 2 * which + half
                value = jnp.where(piece == 2 * core + half, place, -1)
                out_ref[at : at + 1, k * 128 : (k + 1) * 128] = value


def batch_slots(core, batch_index, nys_index):
    vmem = pl.BlockSpec(memory_space=pltpu.VMEM)
    return pl.pallas_call(
        batch_slots_kernel,
        in_specs=[pl.BlockSpec(memory_space=pltpu.SMEM), vmem, vmem],
        out_shape=jax.ShapeDtypeStruct((4, BATCH), jnp.int32),
        compiler_params=params(grid=0),
        cost_estimate=cost(1e6, MIB),
        name="batch_slots",
    )(core, batch_index, nys_index)


def unpack_batch_kernel(slot_ref, own_ref, other_ref, left_ref, right_ref):
    chips = 64
    rows = chips * SLOTROWS
    total = jnp.zeros((3 * FEATS, BATCH), F32)
    for which, ref in ((0, own_ref), (1, other_ref)):
        for part in range(NCHIPS // chips):
            block = ref[part * chips : (part + 1) * chips].reshape(rows, 128).T
            hi, mid, low = split3(block)
            place = lax.broadcasted_iota(jnp.int32, (rows, BATCH), 0) + part * rows
            for half in range(2):
                at = slice(half * FEATS, (half + 1) * FEATS)
                parts = jnp.concatenate([hi[at], mid[at], low[at]], axis=0).astype(BF16)
                slot = slot_ref[2 * which + half : 2 * which + half + 1]
                total += dot(parts, jnp.where(place == slot, 1.0, 0.0).astype(BF16))
    feats = total[:FEATS] + total[FEATS : 2 * FEATS] + total[2 * FEATS :]
    left_ref[...] = left_side(feats.T)
    right_ref[...] = right_side(feats)


def unpack_batch(slots, own, other):
    return pl.pallas_call(
        unpack_batch_kernel,
        out_shape=[
            jax.ShapeDtypeStruct((BATCH, DEPTH), BF16),
            jax.ShapeDtypeStruct((DEPTH, BATCH), BF16),
        ],
        compiler_params=params(grid=0),
        cost_estimate=cost(1e9, 4 * MIB),
        name="unpack_batch",
    )(slots, own, other)


def unpack_nys_kernel(core_ref, start_ref, own_ref, other_ref, out_ref, held):
    n = SLOTROWS

    def run(zero_ref, one_ref):
        def body(i, _):
            at = start_ref[i]
            zero, one = zero_ref[i], one_ref[i]
            held[pl.ds(at, n), :] = zero[:, :FEATS]
            held[pl.ds(at + n, n), :] = zero[:, FEATS:]
            held[pl.ds(at + 2 * n, n), :] = one[:, :FEATS]
            held[pl.ds(at + 3 * n, n), :] = one[:, FEATS:]
            return 0

        lax.fori_loop(0, NCHIPS, body, 0, unroll=8)

    @pl.when(core_ref[0] == 0)
    def _():
        run(own_ref, other_ref)

    @pl.when(core_ref[0] == 1)
    def _():
        run(other_ref, own_ref)

    width = 512
    for i in range(NYS // width):
        at = slice(i * width, (i + 1) * width)
        out_ref[at, :] = left_side(held[at, :])


def unpack_nys(core, starts, own, other):
    smem = pl.BlockSpec(memory_space=pltpu.SMEM)
    vmem = pl.BlockSpec(memory_space=pltpu.VMEM)
    return pl.pallas_call(
        unpack_nys_kernel,
        in_specs=[smem, smem, vmem, vmem],
        out_shape=jax.ShapeDtypeStruct((NYS, DEPTH), BF16),
        scratch_shapes=[pltpu.VMEM((NYS + SLOTS, FEATS), F32)],
        compiler_params=params(grid=0),
        cost_estimate=cost(0, 8 * MIB),
        name="unpack_nys",
    )(core, starts, own, other)


def order_kernel(index_ref, out_ref):
    chip = chip_of(index_ref[...])
    chips = lax.broadcasted_iota(jnp.int32, (NCHIPS, NYS), 0)
    member = jnp.where(chips == chip, 1.0, 0.0)
    lower = lax.broadcasted_iota(jnp.int32, (128, 128), 0)
    upper = lax.broadcasted_iota(jnp.int32, (128, 128), 1)
    counts = jnp.sum(member, axis=1, keepdims=True)
    start = jnp.dot(
        jnp.where(upper < lower, 1.0, 0.0),
        jnp.broadcast_to(counts, (NCHIPS, 128)),
        precision=lax.Precision.HIGHEST,
        preferred_element_type=F32,
    )
    earlier = jnp.where(lower < upper, 1.0, 0.0).astype(BF16)
    for k in range(NYS // 128):
        block = member[:, k * 128 : (k + 1) * 128]
        place = dot(block.astype(BF16), earlier) + start
        place = jnp.sum(block * place, axis=0, keepdims=True)
        out_ref[:, k * 128 : (k + 1) * 128] = place.astype(jnp.int32)
        start = start + jnp.sum(block, axis=1, keepdims=True)


def order(index):
    return pl.pallas_call(
        order_kernel,
        out_shape=jax.ShapeDtypeStruct((1, NYS), jnp.int32),
        compiler_params=params(grid=0),
        cost_estimate=cost(1e9, 4 * MIB),
        name="order",
    )(index)


def reorder_kernel(row_ref, order_ref, eig0, eig1, eig2, eig3, out_ref, parts):
    width = out_ref.shape[1]
    step = pl.program_id(0)
    block = NYS // NROW

    @pl.when(step == 0)
    def _():
        for i in range(NROW):
            at = pl.multiple_of((row_ref[0] ^ i) * block, block)
            hi, mid, low = split3((eig0, eig1, eig2, eig3)[i // 2][i % 2])
            parts[:, pl.ds(at, block)] = jnp.concatenate([hi, mid, low], axis=0).astype(BF16)

    place = lax.broadcasted_iota(jnp.int32, (width, NYS), 0) + step * width
    chosen = jnp.where(place == order_ref[...], 1.0, 0.0).astype(BF16)
    got = dot_nt(parts[...], chosen)
    out_ref[...] = got[:MODES] + got[MODES : 2 * MODES] + got[2 * MODES :]


def reorder(row, orders, eig):
    block = 256
    return pl.pallas_call(
        reorder_kernel,
        grid=(NYS // block,),
        in_specs=[
            pl.BlockSpec(memory_space=pltpu.SMEM),
            pl.BlockSpec((1, NYS), lambda i: (0, 0)),
        ]
        + [pl.BlockSpec((2, MODES, NYS // NROW), lambda i: (0, 0, 0))] * 4,
        out_specs=pl.BlockSpec((MODES, block), lambda i: (0, i)),
        out_shape=jax.ShapeDtypeStruct((MODES, NYS), F32),
        scratch_shapes=[pltpu.VMEM((3 * MODES, NYS), BF16)],
        compiler_params=params(),
        cost_estimate=cost(1e10, 2 * MIB),
        name="reorder",
    )(row, orders, *eig)


def add_spread_kernel(in_ref, out_ref):
    total = in_ref[0]
    for i in range(1, in_ref.shape[0]):
        total = total + in_ref[i]
    for i in range(out_ref.shape[0]):
        out_ref[i] = total


def add_spread(parts, copies):
    return pl.pallas_call(
        add_spread_kernel,
        out_shape=jax.ShapeDtypeStruct((copies,) + parts.shape[1:], F32),
        compiler_params=params(grid=0),
        cost_estimate=cost(parts.size, parts.size * 4 + parts.size // parts.shape[0] * copies * 4),
        name="add_spread",
    )(parts)


def place_tiles(core_ref, own_ref, other_ref, out_ref):
    mine = core_ref[0]
    for x in range(NX):
        for part, core in ((own_ref, mine), (other_ref, 1 - mine)):
            at = pl.multiple_of((2 * x + core) * 8, 8)
            for c in range(NCOL):
                out_ref[pl.ds(at, 8), c * 128 : (c + 1) * 128] = part[x * NCOL + c]


def call(body, name, out_shape, *args, flops=1e9, nbytes=MIB, trans=0):
    spaces = [pltpu.SMEM if a.size == 1 else pltpu.VMEM for a in args]
    many = isinstance(out_shape, list)
    out = pl.BlockSpec(memory_space=pltpu.VMEM)
    return pl.pallas_call(
        body,
        in_specs=[pl.BlockSpec(memory_space=m) for m in spaces],
        out_specs=[out] * len(out_shape) if many else out,
        out_shape=out_shape,
        compiler_params=params(grid=0),
        cost_estimate=cost(flops, nbytes, trans),
        name=name,
    )(*args)


def sides_kernel(cent_ref, left_ref, right_ref):
    width = 512
    for i in range(cent_ref.shape[1] // width):
        at = slice(i * width, (i + 1) * width)
        left_ref[at, :] = left_side(cent_ref[:, at].T)
        right_ref[:, at] = right_side(cent_ref[:, at])


def sides(feats):
    n = feats.shape[1]
    shapes = [
        jax.ShapeDtypeStruct((n, DEPTH), BF16),
        jax.ShapeDtypeStruct((DEPTH, n), BF16),
    ]
    return call(sides_kernel, "sides", shapes, feats, nbytes=5 * MIB)


def batch_kernel(left_ref, right_ref, wts_ref, pred_ref):
    width = 512
    total = jnp.zeros((2 * OUTS, BATCH), F32)
    rest = jnp.zeros((OUTS, BATCH), F32)
    for i in range(PDEV // width):
        at = slice(i * width, (i + 1) * width)
        khi, klo = split2(kern(left_ref[at, :], right_ref[...]))
        whi, wlo = split2(wts_ref[:, at])
        total += dot(jnp.concatenate([whi, wlo], axis=0), khi)
        rest += dot(whi, klo)
    pred_ref[...] = total[:OUTS] + total[OUTS:] + rest


def batch_products(cent_left, batch_right, wts_t):
    return call(
        batch_kernel,
        "batch_products",
        jax.ShapeDtypeStruct((OUTS, BATCH), F32),
        cent_left,
        batch_right,
        wts_t,
        flops=6e9,
        nbytes=2 * MIB,
        trans=PDEV * BATCH,
    )


def modes_kernel(right_ref, nys_ref, eig_ref, scale_ref, out_ref):
    width = 512
    total = jnp.zeros((2 * MODES, BATCH), F32)
    for i in range(NYS // width):
        at = slice(i * width, (i + 1) * width)
        khi, klo = split2(kern(nys_ref[at, :], right_ref[...]))
        ehi, elo = split2(eig_ref[:, at])
        eig = jnp.concatenate([ehi, elo], axis=0)
        total += dot(eig, khi) + dot(eig, klo)
    out_ref[...] = (total[:MODES] + total[MODES:]) * scale_ref[...]


def mode_products(batch_right, nys_left, eig, scale):
    return call(
        modes_kernel,
        "mode_products",
        jax.ShapeDtypeStruct((MODES, BATCH), F32),
        batch_right,
        nys_left,
        eig,
        scale,
        flops=1e10,
        nbytes=5 * MIB,
        trans=NYS * BATCH,
    )


def nys_kernel(nys_ref, right_ref, hi_ref, lo_ref):
    khi, klo = split2(kern(nys_ref[...], right_ref[...]))
    hi_ref[...] = khi
    lo_ref[...] = klo


def nys_parts(cent_right, nys_left, part):
    rows = 512
    count = NYS // PARTS
    shape = jax.ShapeDtypeStruct((count, PDEV), BF16)
    return pl.pallas_call(
        nys_kernel,
        grid=(count // rows,),
        in_specs=[
            pl.BlockSpec((rows, DEPTH), lambda i: (i + part * (count // rows), 0)),
            pl.BlockSpec((DEPTH, PDEV), lambda i: (0, 0)),
        ],
        out_specs=[pl.BlockSpec((rows, PDEV), lambda i: (i, 0))] * 2,
        out_shape=[shape, shape],
        compiler_params=params(56),
        cost_estimate=cost(1.8e10 / PARTS, 34 * MIB / PARTS, PDEV * NYS / PARTS),
        name="nys_parts",
    )(nys_left, cent_right)


def correct_kernel(pred_ref, targ_ref, modes_ref, eig_ref, resid_ref, tiles_ref):
    total = pred_ref[0]
    for i in range(1, NCOL):
        total = total + pred_ref[i]
    resid = total - targ_ref[...]
    resid_ref[...] = resid
    coeff = lax.dot_general(
        resid,
        modes_ref[...],
        (((1,), (1,)), ((), ())),
        precision=lax.Precision.HIGHEST,
        preferred_element_type=F32,
    )
    share = jnp.dot(
        coeff, eig_ref[...], precision=lax.Precision.HIGHEST, preferred_element_type=F32
    )
    for k in range(NCOL):
        tiles_ref[k] = share[:, k * 128 : (k + 1) * 128]


def correct(pred, targ, modes, eig):
    return pl.pallas_call(
        correct_kernel,
        out_shape=[
            jax.ShapeDtypeStruct((8, BATCH), F32),
            jax.ShapeDtypeStruct((NCOL, 8, 128), F32),
        ],
        compiler_params=params(grid=0),
        cost_estimate=cost(1e8, 2 * MIB),
        name="correct",
    )(pred, targ, modes, eig)


def direct_kernel(row_ref, left_ref, right_ref, res0, res1, res2, res3, out_ref, outr_ref):
    for i in range(NROW):
        at = pl.multiple_of((row_ref[0] ^ i) * 8, 8)
        outr_ref[pl.ds(at, 8), :] = (res0, res1, res2, res3)[i // 2][i % 2]
    parts = jnp.concatenate(split2(outr_ref[...]), axis=0)
    width = 512
    for i in range(PDEV // width):
        at = slice(i * width, (i + 1) * width)
        khi, klo = split2(kern(left_ref[...], right_ref[:, at]))
        both = dot(parts, khi) + dot(parts, klo)
        out_ref[:, at] = both[:OUTS] + both[OUTS:]


def direct_part(row, batch_left, cent_right, resid):
    shapes = [
        jax.ShapeDtypeStruct((OUTS, PDEV), F32),
        jax.ShapeDtypeStruct((OUTS, BATCH), F32),
    ]
    return call(
        direct_kernel,
        "direct_part",
        shapes,
        row,
        batch_left,
        cent_right,
        *resid,
        flops=6e9,
        nbytes=3 * MIB,
        trans=PDEV * BATCH,
    )


def step_kernel(core_ref, own_ref, other_ref, direct_ref, *refs):
    his, los = refs[0 : 2 * PARTS : 2], refs[1 : 2 * PARTS : 2]
    out_ref, corr, parts, total = refs[2 * PARTS :]
    step = pl.program_id(0)
    rows = his[0].shape[0]

    @pl.when(step == 0)
    def _():
        place_tiles(core_ref, own_ref, other_ref, corr)
        hi, lo = split2(corr[...])
        parts[:OUTS] = hi
        parts[OUTS:] = lo

    steps = NYS // PARTS // rows
    more = jnp.zeros(total.shape, F32)
    for i in range(PARTS):
        first = pl.multiple_of((i * steps + step) * rows, rows)
        coeff = parts[:, pl.ds(first, rows)]
        more += dot(coeff, his[i][...]) + dot(coeff, los[i][...])

    @pl.when(step == 0)
    def _():
        total[...] = more

    @pl.when(step > 0)
    def _():
        total[...] += more

    @pl.when(step == pl.num_programs(0) - 1)
    def _():
        out_ref[...] = RATE * (direct_ref[...] - (total[:OUTS] + total[OUTS:]))


def step_of(core, own, other, matrices, direct):
    rows = 256
    whole = pl.BlockSpec((NCHIPS, 8, 128), lambda i: (0, 0, 0))
    matrix = pl.BlockSpec((rows, PDEV), lambda i: (i, 0))
    return pl.pallas_call(
        step_kernel,
        grid=(NYS // PARTS // rows,),
        in_specs=[
            pl.BlockSpec(memory_space=pltpu.SMEM),
            whole,
            whole,
            pl.BlockSpec((OUTS, PDEV), lambda i: (0, 0)),
        ]
        + [matrix] * (2 * PARTS),
        out_specs=pl.BlockSpec((OUTS, PDEV), lambda i: (0, 0)),
        out_shape=jax.ShapeDtypeStruct((OUTS, PDEV), F32),
        scratch_shapes=[
            pltpu.VMEM((OUTS, NYS), F32),
            pltpu.VMEM((2 * OUTS, NYS), BF16),
            pltpu.VMEM((2 * OUTS, PDEV), F32),
        ],
        compiler_params=params(56),
        cost_estimate=cost(1.2e10, 36 * MIB),
        name="step_of",
    )(core, own, other, direct, *matrices)


def swap(parts, axes):
    return lax.all_to_all(parts, axes, 0, 0, tiled=True)


def other_core(block):
    return lax.ppermute(block, "core", [(0, 1), (1, 0)])


def pair_kernel(one_ref, two_ref, out_ref):
    out_ref[0] = one_ref[...]
    out_ref[1] = two_ref[...]


def over_row(block):
    shape = jax.ShapeDtypeStruct((2,) + block.shape, F32)
    held = call(pair_kernel, "pair", shape, block, other_core(block))
    flips = [[(i, i ^ flip) for i in range(NX)] for flip in (1, 2, 3)]
    return [held] + [lax.ppermute(held, "x", pairs) for pairs in flips]


def after(value, *first):
    return lax.optimization_barrier((value,) + first)[0]


def finish(core, row, cent, wts_t, targ, scale, batch, get_nys, eig):
    cent_left, cent_right = cent
    batch_left, batch_right = batch
    pred = batch_products(cent_left, batch_right, wts_t).reshape(NROW, 8, BATCH)
    nys = get_nys(pred)
    pred = add_spread(after(swap(pred, ROW), nys), NCOL)

    modes = mode_products(batch_right, after(nys, pred), eig, scale)
    resid, tiles = correct(after(swap(pred, COL), modes), targ, modes, eig)

    one = nys_parts(cent_right, after(nys, tiles), 0)
    tiles = add_spread(after(swap(tiles, COL), *one), NCHIPS)

    two = nys_parts(cent_right, after(nys, tiles), 1)
    direct, resid_t = direct_part(row, batch_left, cent_right, over_row(after(resid, tiles)))
    own = after(swap(tiles, CHIPS), direct, *two)
    step_t = step_of(core, own, other_core(own), one + two, direct)
    return resid_t.T, step_t.T


def slotted(centres, weights, targets, batch_index, nystrom_index, eigvecs, mode_scale):
    core = jnp.full((1,), lax.axis_index("core"), jnp.int32)
    row = jnp.full((1,), lax.axis_index(ROW), jnp.int32)
    chip = jnp.full((1,), lax.axis_index(CHIPS), jnp.int32)
    cent_t = centres.T

    index = jnp.concatenate([nystrom_index, batch_index])
    keep, send = pack(core, chip, index.reshape(-1, 128), cent_t)
    message = join_spread(keep, other_core(send))

    index = after(index, message)
    chips = jnp.arange(NCHIPS, dtype=jnp.int32)[:, None]
    owner = chip_of(index)[None, :]
    fits = jnp.max(jnp.sum((owner == chips).astype(jnp.int32), axis=1)) <= SLOTS
    starts = jnp.sum((owner[:, :NYS] < chips).astype(jnp.int32), axis=1)
    targ = own_targets(row, targets)
    batch_row, nys_row = index[None, NYS:], index[None, :NYS]
    slots = batch_slots(core, batch_row, nys_row)
    cent = sides(after(cent_t, message, fits, starts, targ))
    eig = reorder(row, order(nys_row), over_row(eigvecs.T))

    own, fits, starts, targ = lax.optimization_barrier(
        (swap(message, CHIPS), fits, starts, targ, slots, *cent, eig)
    )[:4]
    other = other_core(own)
    batch = unpack_batch(slots, own, other)
    result = finish(
        core,
        row,
        cent,
        weights.T,
        targ,
        mode_scale[:, None],
        batch,
        lambda pred: unpack_nys(core, starts, after(own, pred), other),
        eig,
    )
    return fits, result


def own_targets(row, targets):
    return lax.dynamic_slice_in_dim(targets.T, row[0] * 8, 8, 0)


def select_kernel(index_ref, cent_ref, out_ref):
    hi, mid, low = split3(cent_ref[...])
    parts = jnp.concatenate([hi, mid, low], axis=0).astype(BF16)
    place = lax.broadcasted_iota(jnp.int32, (PDEV, out_ref.shape[1]), 0)
    found = dot(parts, jnp.where(place == index_ref[...], 1.0, 0.0).astype(BF16))
    out_ref[...] = found[:FEATS] + found[FEATS : 2 * FEATS] + found[2 * FEATS :]


def select(index, cent_t):
    n = index.shape[1]
    block = 512
    return pl.pallas_call(
        select_kernel,
        grid=(n // block,),
        in_specs=[
            pl.BlockSpec((1, block), lambda i: (0, i)),
            pl.BlockSpec((FEATS, PDEV), lambda i: (0, 0)),
        ],
        out_specs=pl.BlockSpec((FEATS, block), lambda i: (0, i)),
        out_shape=jax.ShapeDtypeStruct((FEATS, n), F32),
        compiler_params=params(),
        cost_estimate=cost(2 * 192 * PDEV * n, PDEV * 256 + n * 256),
        name="select",
    )(index, cent_t)


def gather_rows(index, cent_t):
    n = index.shape[0]
    offset = lax.axis_index(ALL) * PDEV
    feats = swap(select((index - offset)[None, :], cent_t).reshape(NROW, 8, n), ROW)
    feats = jnp.sum(feats, axis=0).reshape(8, NCOL, n // NCOL).swapaxes(0, 1)
    feats = jnp.sum(swap(feats, COL), axis=0)
    feats = swap(jnp.broadcast_to(feats[None], (NCOL, 8, n // NCOL)), COL)
    feats = feats.swapaxes(0, 1).reshape(8, n)
    return swap(jnp.broadcast_to(feats[None], (NROW, 8, n)), ROW).reshape(FEATS, n)


def general(centres, weights, targets, batch_index, nystrom_index, eigvecs, mode_scale):
    core = jnp.full((1,), lax.axis_index("core"), jnp.int32)
    row = jnp.full((1,), lax.axis_index(ROW), jnp.int32)
    cent_t = centres.T
    batch_t = gather_rows(batch_index, cent_t)
    cent = sides(cent_t)
    targ = own_targets(row, targets)
    nys = sides(gather_rows(nystrom_index, cent_t))[0]
    eig = reorder(row, jnp.arange(NYS, dtype=jnp.int32)[None, :], over_row(eigvecs.T))
    return finish(
        core,
        row,
        cent,
        weights.T,
        targ,
        mode_scale[:, None],
        sides(batch_t),
        lambda pred: nys,
        eig,
    )


def local(*args):
    fits, result = slotted(*args)
    return lax.cond(fits, lambda done: done, lambda done: general(*args), result)


def solution(mesh):
    fine = Mesh(mesh.devices.reshape(NX, NCORE, 8, 4), ALL)
    in_specs = (
        P(ALL, None),
        P(ALL, None),
        P(),
        P(),
        P(),
        P(ROW, COL),
        P(COL),
    )
    out_specs = (P(), P(ALL, None))
    return jax.shard_map(local, mesh=fine, in_specs=in_specs, out_specs=out_specs, check_vma=False)
```

```python
import functools

import jax
import jax.numpy as jnp
from jax import lax
from jax.experimental import pallas as pl
from jax.experimental.pallas import tpu as pltpu
from jax.sharding import Mesh
from jax.sharding import PartitionSpec as P

F32 = jnp.float32
BF16 = jnp.bfloat16
ROW = ("x", "core")
COL = ("z", "y")
CHIPS = ("x", "z", "y")
ALL = ("x", "core", "z", "y")
NX, NCORE, NROW, NCOL, NCHIPS = 4, 2, 8, 32, 128
FEATS, OUTS, BATCH, NYS, MODES = 64, 64, 512, 4096, 32
PDEV = 2048
SHIFT = 11
SLOTS, SLOTROWS = 64, 16
PARTS = 2
RATE = 0.25
LOG2E = 1.4426950408889634
DEPTH = 6 * FEATS + 128
MIB = 1024 * 1024


def params(mib=14, grid=1):
    return pltpu.CompilerParams(
        vmem_limit_bytes=mib * MIB, dimension_semantics=("arbitrary",) * grid
    )


def cost(flops, nbytes, trans=0):
    return pl.CostEstimate(flops=int(flops), bytes_accessed=int(nbytes), transcendentals=int(trans))


def dot(a, b):
    return lax.dot_general(a, b, (((1,), (0,)), ((), ())), preferred_element_type=F32)


def dot_nt(a, b):
    return lax.dot_general(a, b, (((1,), (1,)), ((), ())), preferred_element_type=F32)


def split2(v):
    hi = v.astype(BF16)
    lo = (v - hi.astype(F32)).astype(BF16)
    return hi, lo


def split3(v):
    hi = v.astype(BF16).astype(F32)
    rest = v - hi
    mid = rest.astype(BF16).astype(F32)
    low = (rest - mid).astype(BF16).astype(F32)
    return hi, mid, low


def left_side(a):
    ah, am, al = split3(a * (2.0 * LOG2E / FEATS))
    sq = split3(jnp.sum(a * a, axis=1, keepdims=True) * (-LOG2E / FEATS))
    lane = lax.broadcasted_iota(jnp.int32, (a.shape[0], 128), 1)
    extra = jnp.where((lane >= 3) & (lane < 6), 1.0, 0.0)
    for i in range(3):
        extra = jnp.where(lane == i, sq[i], extra)
    return jnp.concatenate([ah, ah, am, am, ah, al, extra], axis=1).astype(BF16)


def right_side(bt):
    bh, bm, bl = split3(bt)
    sq = split3(jnp.sum(bt * bt, axis=0, keepdims=True) * (-LOG2E / FEATS))
    row = lax.broadcasted_iota(jnp.int32, (128, bt.shape[1]), 0)
    extra = jnp.where(row < 3, 1.0, 0.0)
    for i in range(3):
        extra = jnp.where(row == 3 + i, sq[i], extra)
    return jnp.concatenate([bh, bm, bh, bm, bl, bh, extra], axis=0).astype(BF16)


def kern(left, right):
    return jnp.exp2(dot(left, right))


def chip_of(index):
    owner = lax.shift_right_logical(index, SHIFT)
    return lax.shift_right_logical(owner, 6) * NCOL + (owner & (NCOL - 1))


def core_of(index):
    return lax.shift_right_logical(index, SHIFT + 5) & 1


def pack_kernel(core_ref, chip_ref, index_ref, cent_ref, keep_ref, send_ref):
    rows = index_ref.shape[0]
    index = index_ref[...]
    ours = chip_of(index) == chip_ref[0]
    ones = jnp.where(ours, 1.0, 0.0).astype(BF16)
    lane_from = lax.broadcasted_iota(jnp.int32, (128, 128), 0)
    lane_to = lax.broadcasted_iota(jnp.int32, (128, 128), 1)
    in_row = dot(ones, jnp.where(lane_from < lane_to, 1.0, 0.0).astype(BF16))
    row_to = lax.broadcasted_iota(jnp.int32, (rows, rows), 0)
    row_from = lax.broadcasted_iota(jnp.int32, (rows, rows), 1)
    before = dot(jnp.where(row_from < row_to, 1.0, 0.0).astype(BF16), ones)
    rank = in_row + jnp.sum(before, axis=1, keepdims=True)
    rank = jnp.where(ours & (core_of(index) == core_ref[0]), rank, -1.0)
    local_row = (index & (PDEV - 1)).astype(F32) + 1.0

    slot = lax.broadcasted_iota(jnp.int32, (SLOTS, 128), 0).astype(F32)
    found = jnp.zeros((SLOTS, 128), F32)
    for i in range(rows):
        found += jnp.where(rank[i : i + 1] == slot, local_row[i : i + 1], 0.0)
    source = jnp.sum(found, axis=1, keepdims=True).astype(jnp.int32) - 1
    place = lax.broadcasted_iota(jnp.int32, (SLOTS, PDEV), 1)
    chosen = jnp.where(place == source, 1.0, 0.0).astype(BF16)
    hi, mid, low = split3(cent_ref[...])
    parts = jnp.concatenate([hi, mid, low], axis=0).astype(BF16)
    got = dot_nt(chosen, parts)
    got = got[:, :FEATS] + got[:, FEATS : 2 * FEATS] + got[:, 2 * FEATS :]
    n = SLOTROWS
    zero = jnp.concatenate([got[:n], got[n : 2 * n]], axis=1)
    one = jnp.concatenate([got[2 * n : 3 * n], got[3 * n :]], axis=1)
    at_zero = core_ref[0] == 0
    keep_ref[...] = jnp.where(at_zero, zero, one)
    send_ref[...] = jnp.where(at_zero, one, zero)


def pack(core, chip, index, cent_t):
    smem = pl.BlockSpec(memory_space=pltpu.SMEM)
    vmem = pl.BlockSpec(memory_space=pltpu.VMEM)
    shape = jax.ShapeDtypeStruct((SLOTROWS, 128), F32)
    return pl.pallas_call(
        pack_kernel,
        in_specs=[smem, smem, vmem, vmem],
        out_shape=[shape, shape],
        compiler_params=params(grid=0),
        cost_estimate=cost(1e9, 2 * MIB),
        name="pack",
    )(core, chip, index, cent_t)


def join_spread_kernel(keep_ref, came_ref, out_ref):
    message = keep_ref[...] + came_ref[...]
    for i in range(out_ref.shape[0]):
        out_ref[i] = message


def join_spread(keep, came):
    return pl.pallas_call(
        join_spread_kernel,
        out_shape=jax.ShapeDtypeStruct((NCHIPS,) + keep.shape, F32),
        compiler_params=params(grid=0),
        cost_estimate=cost(0, MIB),
        name="join_spread",
    )(keep, came)


def across_rows(row):
    return jnp.broadcast_to(row.astype(F32), (128, row.shape[1])).T


def batch_slots_kernel(core_ref, batch_ref, nys_ref, out_ref):
    index = batch_ref[...]
    chip = chip_of(index)
    source = lax.broadcasted_iota(jnp.int32, (BATCH, 128), 0)
    lane = lax.broadcasted_iota(jnp.int32, (BATCH, 128), 1)
    from_batch = across_rows(chip)
    from_nys = across_rows(chip_of(nys_ref[...]))
    for k in range(BATCH // 128):
        here = chip[:, k * 128 : (k + 1) * 128]
        target = here.astype(F32)
        ahead = (from_batch == target) & (source < lane + k * 128)
        rank = jnp.sum(jnp.where(ahead, 1.0, 0.0), axis=0, keepdims=True)
        rank += jnp.sum(jnp.where(from_nys == target, 1.0, 0.0), axis=0, keepdims=True)
        rank = rank.astype(jnp.int32)
        place = here * SLOTROWS + (rank & (SLOTROWS - 1))
        piece = lax.shift_right_logical(rank, 4)
        for which in range(2):
            core = core_ref[0] if which == 0 else 1 - core_ref[0]
            for half in range(2):
                at = 2 * which + half
                value = jnp.where(piece == 2 * core + half, place, -1)
                out_ref[at : at + 1, k * 128 : (k + 1) * 128] = value


def batch_slots(core, batch_index, nys_index):
    vmem = pl.BlockSpec(memory_space=pltpu.VMEM)
    return pl.pallas_call(
        batch_slots_kernel,
        in_specs=[pl.BlockSpec(memory_space=pltpu.SMEM), vmem, vmem],
        out_shape=jax.ShapeDtypeStruct((4, BATCH), jnp.int32),
        compiler_params=params(grid=0),
        cost_estimate=cost(1e6, MIB),
        name="batch_slots",
    )(core, batch_index, nys_index)


def unpack_batch_kernel(slot_ref, own_ref, other_ref, left_ref, right_ref):
    chips = 64
    rows = chips * SLOTROWS
    total = jnp.zeros((3 * FEATS, BATCH), F32)
    for which, ref in ((0, own_ref), (1, other_ref)):
        for part in range(NCHIPS // chips):
            block = ref[part * chips : (part + 1) * chips].reshape(rows, 128).T
            hi, mid, low = split3(block)
            place = lax.broadcasted_iota(jnp.int32, (rows, BATCH), 0) + part * rows
            for half in range(2):
                at = slice(half * FEATS, (half + 1) * FEATS)
                parts = jnp.concatenate([hi[at], mid[at], low[at]], axis=0).astype(BF16)
                slot = slot_ref[2 * which + half : 2 * which + half + 1]
                total += dot(parts, jnp.where(place == slot, 1.0, 0.0).astype(BF16))
    feats = total[:FEATS] + total[FEATS : 2 * FEATS] + total[2 * FEATS :]
    left_ref[...] = left_side(feats.T)
    right_ref[...] = right_side(feats)


def unpack_batch(slots, own, other):
    return pl.pallas_call(
        unpack_batch_kernel,
        out_shape=[
            jax.ShapeDtypeStruct((BATCH, DEPTH), BF16),
            jax.ShapeDtypeStruct((DEPTH, BATCH), BF16),
        ],
        compiler_params=params(grid=0),
        cost_estimate=cost(1e9, 4 * MIB),
        name="unpack_batch",
    )(slots, own, other)


def unpack_nys_kernel(core_ref, start_ref, own_ref, other_ref, out_ref, held):
    n = SLOTROWS

    def run(zero_ref, one_ref):
        def body(i, _):
            at = start_ref[i]
            zero, one = zero_ref[i], one_ref[i]
            held[pl.ds(at, n), :] = zero[:, :FEATS]
            held[pl.ds(at + n, n), :] = zero[:, FEATS:]
            held[pl.ds(at + 2 * n, n), :] = one[:, :FEATS]
            held[pl.ds(at + 3 * n, n), :] = one[:, FEATS:]
            return 0

        lax.fori_loop(0, NCHIPS, body, 0, unroll=8)

    @pl.when(core_ref[0] == 0)
    def _():
        run(own_ref, other_ref)

    @pl.when(core_ref[0] == 1)
    def _():
        run(other_ref, own_ref)

    out_ref[...] = held[:NYS, :]


def unpack_nys(core, starts, own, other):
    smem = pl.BlockSpec(memory_space=pltpu.SMEM)
    vmem = pl.BlockSpec(memory_space=pltpu.VMEM)
    return pl.pallas_call(
        unpack_nys_kernel,
        in_specs=[smem, smem, vmem, vmem],
        out_shape=jax.ShapeDtypeStruct((NYS, FEATS), F32),
        scratch_shapes=[pltpu.VMEM((NYS + SLOTS, FEATS), F32)],
        compiler_params=params(grid=0),
        cost_estimate=cost(0, 8 * MIB),
        name="unpack_nys",
    )(core, starts, own, other)


def order_kernel(index_ref, out_ref):
    chip = chip_of(index_ref[...])
    chips = lax.broadcasted_iota(jnp.int32, (NCHIPS, NYS), 0)
    member = jnp.where(chips == chip, 1.0, 0.0)
    lower = lax.broadcasted_iota(jnp.int32, (128, 128), 0)
    upper = lax.broadcasted_iota(jnp.int32, (128, 128), 1)
    counts = jnp.sum(member, axis=1, keepdims=True)
    start = jnp.dot(
        jnp.where(upper < lower, 1.0, 0.0),
        jnp.broadcast_to(counts, (NCHIPS, 128)),
        precision=lax.Precision.HIGHEST,
        preferred_element_type=F32,
    )
    earlier = jnp.where(lower < upper, 1.0, 0.0).astype(BF16)
    for k in range(NYS // 128):
        block = member[:, k * 128 : (k + 1) * 128]
        place = dot(block.astype(BF16), earlier) + start
        place = jnp.sum(block * place, axis=0, keepdims=True)
        out_ref[:, k * 128 : (k + 1) * 128] = place.astype(jnp.int32)
        start = start + jnp.sum(block, axis=1, keepdims=True)


def order(index):
    return pl.pallas_call(
        order_kernel,
        out_shape=jax.ShapeDtypeStruct((1, NYS), jnp.int32),
        compiler_params=params(grid=0),
        cost_estimate=cost(1e9, 4 * MIB),
        name="order",
    )(index)


def reorder_kernel(row_ref, order_ref, eig0, eig1, eig2, eig3, out_ref, parts):
    width = out_ref.shape[1]
    step = pl.program_id(0)
    block = NYS // NROW

    @pl.when(step == 0)
    def _():
        for i in range(NROW):
            at = pl.multiple_of((row_ref[0] ^ i) * block, block)
            hi, mid, low = split3((eig0, eig1, eig2, eig3)[i // 2][i % 2])
            parts[:, pl.ds(at, block)] = jnp.concatenate([hi, mid, low], axis=0).astype(BF16)

    place = lax.broadcasted_iota(jnp.int32, (width, NYS), 0) + step * width
    chosen = jnp.where(place == order_ref[...], 1.0, 0.0).astype(BF16)
    got = dot_nt(parts[...], chosen)
    out_ref[...] = got[:MODES] + got[MODES : 2 * MODES] + got[2 * MODES :]


def reorder(row, orders, eig):
    block = 256
    return pl.pallas_call(
        reorder_kernel,
        grid=(NYS // block,),
        in_specs=[
            pl.BlockSpec(memory_space=pltpu.SMEM),
            pl.BlockSpec((1, NYS), lambda i: (0, 0)),
        ]
        + [pl.BlockSpec((2, MODES, NYS // NROW), lambda i: (0, 0, 0))] * 4,
        out_specs=pl.BlockSpec((MODES, block), lambda i: (0, i)),
        out_shape=jax.ShapeDtypeStruct((MODES, NYS), F32),
        scratch_shapes=[pltpu.VMEM((3 * MODES, NYS), BF16)],
        compiler_params=params(),
        cost_estimate=cost(1e10, 2 * MIB),
        name="reorder",
    )(row, orders, *eig)


def add_spread_kernel(in_ref, out_ref):
    total = in_ref[0]
    for i in range(1, in_ref.shape[0]):
        total = total + in_ref[i]
    for i in range(out_ref.shape[0]):
        out_ref[i] = total


def add_spread(parts, copies):
    return pl.pallas_call(
        add_spread_kernel,
        out_shape=jax.ShapeDtypeStruct((copies,) + parts.shape[1:], F32),
        compiler_params=params(grid=0),
        cost_estimate=cost(parts.size, parts.size * 4 + parts.size // parts.shape[0] * copies * 4),
        name="add_spread",
    )(parts)


def place_tiles(core_ref, own_ref, other_ref, out_ref):
    mine = core_ref[0]
    for x in range(NX):
        for part, core in ((own_ref, mine), (other_ref, 1 - mine)):
            at = pl.multiple_of((2 * x + core) * 8, 8)
            for c in range(NCOL):
                out_ref[pl.ds(at, 8), c * 128 : (c + 1) * 128] = part[x * NCOL + c]


def call(body, name, out_shape, *args, flops=1e9, nbytes=MIB, trans=0):
    spaces = [pltpu.SMEM if a.size == 1 else pltpu.VMEM for a in args]
    many = isinstance(out_shape, list)
    out = pl.BlockSpec(memory_space=pltpu.VMEM)
    return pl.pallas_call(
        body,
        in_specs=[pl.BlockSpec(memory_space=m) for m in spaces],
        out_specs=[out] * len(out_shape) if many else out,
        out_shape=out_shape,
        compiler_params=params(grid=0),
        cost_estimate=cost(flops, nbytes, trans),
        name=name,
    )(*args)


def sides_kernel(cent_ref, left_ref, right_ref):
    width = 512
    for i in range(cent_ref.shape[1] // width):
        at = slice(i * width, (i + 1) * width)
        left_ref[at, :] = left_side(cent_ref[:, at].T)
        right_ref[:, at] = right_side(cent_ref[:, at])


def sides(feats):
    n = feats.shape[1]
    shapes = [
        jax.ShapeDtypeStruct((n, DEPTH), BF16),
        jax.ShapeDtypeStruct((DEPTH, n), BF16),
    ]
    return call(sides_kernel, "sides", shapes, feats, nbytes=5 * MIB)


def lefts_kernel(rows_ref, out_ref):
    width = 512
    for i in range(NYS // width):
        at = slice(i * width, (i + 1) * width)
        out_ref[at, :] = left_side(rows_ref[at, :])


def lefts(rows):
    shape = jax.ShapeDtypeStruct((NYS, DEPTH), BF16)
    return call(lefts_kernel, "lefts", shape, rows, nbytes=6 * MIB)


def batch_kernel(left_ref, right_ref, wts_ref, pred_ref):
    width = 512
    total = jnp.zeros((2 * OUTS, BATCH), F32)
    rest = jnp.zeros((OUTS, BATCH), F32)
    for i in range(PDEV // width):
        at = slice(i * width, (i + 1) * width)
        khi, klo = split2(kern(left_ref[at, :], right_ref[...]))
        whi, wlo = split2(wts_ref[:, at])
        total += dot(jnp.concatenate([whi, wlo], axis=0), khi)
        rest += dot(whi, klo)
    pred_ref[...] = total[:OUTS] + total[OUTS:] + rest


def batch_products(cent_left, batch_right, wts_t):
    return call(
        batch_kernel,
        "batch_products",
        jax.ShapeDtypeStruct((OUTS, BATCH), F32),
        cent_left,
        batch_right,
        wts_t,
        flops=6e9,
        nbytes=2 * MIB,
        trans=PDEV * BATCH,
    )


def modes_kernel(right_ref, nys_ref, eig_ref, scale_ref, out_ref):
    width = 512
    total = jnp.zeros((2 * MODES, BATCH), F32)
    for i in range(NYS // width):
        at = slice(i * width, (i + 1) * width)
        khi, klo = split2(kern(nys_ref[at, :], right_ref[...]))
        ehi, elo = split2(eig_ref[:, at])
        eig = jnp.concatenate([ehi, elo], axis=0)
        total += dot(eig, khi) + dot(eig, klo)
    out_ref[...] = (total[:MODES] + total[MODES:]) * scale_ref[...]


def mode_products(batch_right, nys_left, eig, scale):
    return call(
        modes_kernel,
        "mode_products",
        jax.ShapeDtypeStruct((MODES, BATCH), F32),
        batch_right,
        nys_left,
        eig,
        scale,
        flops=1e10,
        nbytes=5 * MIB,
        trans=NYS * BATCH,
    )


def nys_kernel(nys_ref, right_ref, hi_ref, lo_ref):
    khi, klo = split2(kern(nys_ref[...], right_ref[...]))
    hi_ref[...] = khi
    lo_ref[...] = klo


def nys_parts(cent_right, nys_left, part):
    rows = 512
    count = NYS // PARTS
    shape = jax.ShapeDtypeStruct((count, PDEV), BF16)
    return pl.pallas_call(
        nys_kernel,
        grid=(count // rows,),
        in_specs=[
            pl.BlockSpec((rows, DEPTH), lambda i: (i + part * (count // rows), 0)),
            pl.BlockSpec((DEPTH, PDEV), lambda i: (0, 0)),
        ],
        out_specs=[pl.BlockSpec((rows, PDEV), lambda i: (i, 0))] * 2,
        out_shape=[shape, shape],
        compiler_params=params(56),
        cost_estimate=cost(1.8e10 / PARTS, 34 * MIB / PARTS, PDEV * NYS / PARTS),
        name="nys_parts",
    )(nys_left, cent_right)


def correct_kernel(pred_ref, targ_ref, modes_ref, eig_ref, resid_ref, tiles_ref):
    total = pred_ref[0]
    for i in range(1, NCOL):
        total = total + pred_ref[i]
    resid = total - targ_ref[...]
    resid_ref[...] = resid
    coeff = lax.dot_general(
        resid,
        modes_ref[...],
        (((1,), (1,)), ((), ())),
        precision=lax.Precision.HIGHEST,
        preferred_element_type=F32,
    )
    share = jnp.dot(
        coeff, eig_ref[...], precision=lax.Precision.HIGHEST, preferred_element_type=F32
    )
    for k in range(NCOL):
        tiles_ref[k] = share[:, k * 128 : (k + 1) * 128]


def correct(pred, targ, modes, eig):
    return pl.pallas_call(
        correct_kernel,
        out_shape=[
            jax.ShapeDtypeStruct((8, BATCH), F32),
            jax.ShapeDtypeStruct((NCOL, 8, 128), F32),
        ],
        compiler_params=params(grid=0),
        cost_estimate=cost(1e8, 2 * MIB),
        name="correct",
    )(pred, targ, modes, eig)


def direct_kernel(row_ref, left_ref, right_ref, res0, res1, res2, res3, out_ref, outr_ref):
    for i in range(NROW):
        at = pl.multiple_of((row_ref[0] ^ i) * 8, 8)
        outr_ref[pl.ds(at, 8), :] = (res0, res1, res2, res3)[i // 2][i % 2]
    parts = jnp.concatenate(split2(outr_ref[...]), axis=0)
    width = 512
    for i in range(PDEV // width):
        at = slice(i * width, (i + 1) * width)
        khi, klo = split2(kern(left_ref[...], right_ref[:, at]))
        both = dot(parts, khi) + dot(parts, klo)
        out_ref[:, at] = both[:OUTS] + both[OUTS:]


def direct_part(row, batch_left, cent_right, resid):
    shapes = [
        jax.ShapeDtypeStruct((OUTS, PDEV), F32),
        jax.ShapeDtypeStruct((OUTS, BATCH), F32),
    ]
    return call(
        direct_kernel,
        "direct_part",
        shapes,
        row,
        batch_left,
        cent_right,
        *resid,
        flops=6e9,
        nbytes=3 * MIB,
        trans=PDEV * BATCH,
    )


def step_kernel(core_ref, own_ref, other_ref, direct_ref, *refs):
    his, los = refs[0 : 2 * PARTS : 2], refs[1 : 2 * PARTS : 2]
    out_ref, corr, parts, total = refs[2 * PARTS :]
    step = pl.program_id(0)
    rows = his[0].shape[0]

    @pl.when(step == 0)
    def _():
        place_tiles(core_ref, own_ref, other_ref, corr)
        hi, lo = split2(corr[...])
        parts[:OUTS] = hi
        parts[OUTS:] = lo

    steps = NYS // PARTS // rows
    more = jnp.zeros(total.shape, F32)
    for i in range(PARTS):
        first = pl.multiple_of((i * steps + step) * rows, rows)
        coeff = parts[:, pl.ds(first, rows)]
        more += dot(coeff, his[i][...]) + dot(coeff, los[i][...])

    @pl.when(step == 0)
    def _():
        total[...] = more

    @pl.when(step > 0)
    def _():
        total[...] += more

    @pl.when(step == pl.num_programs(0) - 1)
    def _():
        out_ref[...] = RATE * (direct_ref[...] - (total[:OUTS] + total[OUTS:]))


def step_of(core, own, other, matrices, direct):
    rows = 256
    whole = pl.BlockSpec((NCHIPS, 8, 128), lambda i: (0, 0, 0))
    matrix = pl.BlockSpec((rows, PDEV), lambda i: (i, 0))
    return pl.pallas_call(
        step_kernel,
        grid=(NYS // PARTS // rows,),
        in_specs=[
            pl.BlockSpec(memory_space=pltpu.SMEM),
            whole,
            whole,
            pl.BlockSpec((OUTS, PDEV), lambda i: (0, 0)),
        ]
        + [matrix] * (2 * PARTS),
        out_specs=pl.BlockSpec((OUTS, PDEV), lambda i: (0, 0)),
        out_shape=jax.ShapeDtypeStruct((OUTS, PDEV), F32),
        scratch_shapes=[
            pltpu.VMEM((OUTS, NYS), F32),
            pltpu.VMEM((2 * OUTS, NYS), BF16),
            pltpu.VMEM((2 * OUTS, PDEV), F32),
        ],
        compiler_params=params(56),
        cost_estimate=cost(1.2e10, 36 * MIB),
        name="step_of",
    )(core, own, other, direct, *matrices)


def swap(parts, axes):
    return lax.all_to_all(parts, axes, 0, 0, tiled=True)


def other_core(block):
    return lax.ppermute(block, "core", [(0, 1), (1, 0)])


def pair_kernel(one_ref, two_ref, out_ref):
    out_ref[0] = one_ref[...]
    out_ref[1] = two_ref[...]


def over_row(block):
    shape = jax.ShapeDtypeStruct((2,) + block.shape, F32)
    held = call(pair_kernel, "pair", shape, block, other_core(block))
    flips = [[(i, i ^ flip) for i in range(NX)] for flip in (1, 2, 3)]
    return [held] + [lax.ppermute(held, "x", pairs) for pairs in flips]


def after(value, *first):
    return lax.optimization_barrier((value,) + first)[0]


def finish(core, row, cent, wts_t, targ, scale, batch, get_nys, eig):
    cent_left, cent_right = cent
    batch_left, batch_right = batch
    pred = batch_products(cent_left, batch_right, wts_t).reshape(NROW, 8, BATCH)
    nys = get_nys(pred)
    pred = add_spread(after(swap(pred, ROW), nys), NCOL)

    nys = lefts(after(nys, pred))
    modes = mode_products(batch_right, nys, eig, scale)
    resid, tiles = correct(after(swap(pred, COL), modes), targ, modes, eig)

    one = nys_parts(cent_right, after(nys, tiles), 0)
    tiles = add_spread(after(swap(tiles, COL), *one), NCHIPS)

    two = nys_parts(cent_right, after(nys, tiles), 1)
    direct, resid_t = direct_part(row, batch_left, cent_right, over_row(after(resid, tiles)))
    own = after(swap(tiles, CHIPS), direct, *two)
    step_t = step_of(core, own, other_core(own), one + two, direct)
    return resid_t.T, step_t.T


def slotted(centres, weights, targets, batch_index, nystrom_index, eigvecs, mode_scale):
    core = jnp.full((1,), lax.axis_index("core"), jnp.int32)
    row = jnp.full((1,), lax.axis_index(ROW), jnp.int32)
    chip = jnp.full((1,), lax.axis_index(CHIPS), jnp.int32)
    cent_t = centres.T

    index = jnp.concatenate([nystrom_index, batch_index])
    keep, send = pack(core, chip, index.reshape(-1, 128), cent_t)
    message = join_spread(keep, other_core(send))

    index = after(index, message)
    chips = jnp.arange(NCHIPS, dtype=jnp.int32)[:, None]
    owner = chip_of(index)[None, :]
    fits = jnp.max(jnp.sum((owner == chips).astype(jnp.int32), axis=1)) <= SLOTS
    starts = jnp.sum((owner[:, :NYS] < chips).astype(jnp.int32), axis=1)
    targ = own_targets(row, targets)
    batch_row, nys_row = index[None, NYS:], index[None, :NYS]
    slots = batch_slots(core, batch_row, nys_row)
    eig = reorder(row, order(nys_row), over_row(eigvecs.T))

    own, fits, starts, targ = lax.optimization_barrier(
        (swap(message, CHIPS), fits, starts, targ, slots, eig)
    )[:4]
    other = other_core(own)
    cent = sides(after(cent_t, own))
    batch = unpack_batch(slots, own, other)
    result = finish(
        core,
        row,
        cent,
        weights.T,
        targ,
        mode_scale[:, None],
        batch,
        lambda pred: unpack_nys(core, starts, after(own, pred), other),
        eig,
    )
    return fits, result


def own_targets(row, targets):
    return lax.dynamic_slice_in_dim(targets.T, row[0] * 8, 8, 0)


def select_kernel(index_ref, cent_ref, out_ref):
    hi, mid, low = split3(cent_ref[...])
    parts = jnp.concatenate([hi, mid, low], axis=0).astype(BF16)
    place = lax.broadcasted_iota(jnp.int32, (PDEV, out_ref.shape[1]), 0)
    found = dot(parts, jnp.where(place == index_ref[...], 1.0, 0.0).astype(BF16))
    out_ref[...] = found[:FEATS] + found[FEATS : 2 * FEATS] + found[2 * FEATS :]


def select(index, cent_t):
    n = index.shape[1]
    block = 512
    return pl.pallas_call(
        select_kernel,
        grid=(n // block,),
        in_specs=[
            pl.BlockSpec((1, block), lambda i: (0, i)),
            pl.BlockSpec((FEATS, PDEV), lambda i: (0, 0)),
        ],
        out_specs=pl.BlockSpec((FEATS, block), lambda i: (0, i)),
        out_shape=jax.ShapeDtypeStruct((FEATS, n), F32),
        compiler_params=params(),
        cost_estimate=cost(2 * 192 * PDEV * n, PDEV * 256 + n * 256),
        name="select",
    )(index, cent_t)


def gather_rows(index, cent_t):
    n = index.shape[0]
    offset = lax.axis_index(ALL) * PDEV
    feats = swap(select((index - offset)[None, :], cent_t).reshape(NROW, 8, n), ROW)
    feats = jnp.sum(feats, axis=0).reshape(8, NCOL, n // NCOL).swapaxes(0, 1)
    feats = jnp.sum(swap(feats, COL), axis=0)
    feats = swap(jnp.broadcast_to(feats[None], (NCOL, 8, n // NCOL)), COL)
    feats = feats.swapaxes(0, 1).reshape(8, n)
    return swap(jnp.broadcast_to(feats[None], (NROW, 8, n)), ROW).reshape(FEATS, n)


def general(centres, weights, targets, batch_index, nystrom_index, eigvecs, mode_scale):
    core = jnp.full((1,), lax.axis_index("core"), jnp.int32)
    row = jnp.full((1,), lax.axis_index(ROW), jnp.int32)
    cent_t = centres.T
    batch_t = gather_rows(batch_index, cent_t)
    cent = sides(cent_t)
    targ = own_targets(row, targets)
    nys = gather_rows(nystrom_index, cent_t).T
    eig = reorder(row, jnp.arange(NYS, dtype=jnp.int32)[None, :], over_row(eigvecs.T))
    return finish(
        core,
        row,
        cent,
        weights.T,
        targ,
        mode_scale[:, None],
        sides(batch_t),
        lambda pred: nys,
        eig,
    )


def local(*args):
    fits, result = slotted(*args)
    return lax.cond(fits, lambda done: done, lambda done: general(*args), result)


def solution(mesh):
    fine = Mesh(mesh.devices.reshape(NX, NCORE, 8, 4), ALL)
    in_specs = (
        P(ALL, None),
        P(ALL, None),
        P(),
        P(),
        P(),
        P(ROW, COL),
        P(COL),
    )
    out_specs = (P(), P(ALL, None))
    return jax.shard_map(local, mesh=fine, in_specs=in_specs, out_specs=out_specs, check_vma=False)
```
